32 devices in a mesh: gx: 4 (over z), gy: 4 (over y, x), gz: 2 (over core).
Axes of the slice: x: 2, y: 2, z: 4, core: 2. Of those that a mesh axis runs over, the one named last changes fastest.
Arguments:
- rhs_boxes: float32 [2, 64, 32768], P('gz', ('gx', 'gy')), may hold values from -18 to 18
- a_boxes: float32 [2, 64, 32768], P('gz', ('gx', 'gy')), may hold values from 0.05 to 0.5
- b_boxes: float32 [2, 64, 32768], P('gz', ('gx', 'gy')), may hold values from 0.2 to 2
- new_place: int32 [2, 64], P('gz', ('gx', 'gy')), may hold values from 0 to 63, as said below
Outputs:
- solution: float32 [256, 128, 128], P('gx', 'gy', 'gz')
- residual: float32 [256, 128, 128], P('gx', 'gy', 'gz')
The draws below stay inside these ranges and needn't reach their ends.
Inputs may be any that keep to these rules, and one draw needn't show every extreme that they name: `new_place`: each entry is p = t * 4 + q: the box goes to device t of its layer (counted in the order of the gx+gy axes) at box position q. The entries of one layer are a permutation of its positions. The boxes of one device go to 4 different devices.
All inputs are finite; a program needn't handle non-finite values.
Results may differ from the reference program's by a relative error of at most 0.000079.
Values sent between devices are 32-bit elements; how exact they have to be, the bound alone decides.
A program may use at most 192 MiB of HBM per device.

```python
import math
import jax
import jax.numpy as jnp
from jax import lax

BOX_EDGE = 32
BOXES_Z = 2
SWEEPS = 1
COARSE_SWEEPS = 4
BOX_CELLS = 32768
BOXES_DEV = 4
MEMBERS = 16
LAYERS = 2
NX = 256
NY = 128
NZ = 128
N_GX = 4
N_GY = 4


def layer_places(key):
    subkeys = jax.random.split(key, 4)
    offsets = jax.random.permutation(subkeys[0], MEMBERS)[:BOXES_DEV]
    relabel = jax.random.permutation(subkeys[1], MEMBERS)
    senders = jax.random.permutation(subkeys[2], MEMBERS)
    target = relabel[(senders[:, None] + offsets[None, :]) % MEMBERS]
    position_keys = jax.random.split(subkeys[3], MEMBERS)
    positions = jax.vmap(lambda one_key: jax.random.permutation(one_key, BOXES_DEV))(position_keys)
    landing = positions[target, jnp.arange(BOXES_DEV)[None, :]]
    return (target * BOXES_DEV + landing).reshape(MEMBERS * BOXES_DEV)


def draw_new_place(key, part):
    subkeys = jax.random.split(jax.random.fold_in(key, 11), LAYERS)
    return jax.vmap(layer_places)(subkeys).astype(jnp.int32)


def draw_rhs_boxes(key, part):
    extent = (LAYERS, MEMBERS * BOXES_DEV, BOX_CELLS)
    values = 3.0 * jax.random.normal(jax.random.fold_in(key, 3), extent, jnp.float32)
    return jnp.clip(values, -18.0, 18.0)


def block_levels(stream_key, shape, shards, smallest, largest):
    def one(dim, shards_of):
        heights = jax.random.uniform(jax.random.fold_in(jax.random.fold_in(stream_key, 6), dim), (shards_of,), jnp.float32, smallest / len(shards), largest / len(shards))
        return jnp.repeat(jnp.exp(heights), shape[dim] // shards_of).reshape((-1,) + (1,) * (len(shape) - dim - 1))

    gain = one(*shards[0])
    for cut in shards[1:]:
        gain = gain * one(*cut)
    return gain


def setup_inputs(seed: int = 0) -> dict:
    keys = jax.random.split(jax.random.key(seed), 5)
    rhs_boxes = draw_rhs_boxes(jax.random.fold_in(keys[4], 71), 0)
    a_boxes = jnp.clip(jnp.exp(math.log(0.5) - 2.3025851 * jax.random.uniform(keys[1], (LAYERS, MEMBERS * BOXES_DEV, BOX_CELLS), jnp.float32) ** block_levels(keys[1], (LAYERS, MEMBERS * BOXES_DEV, BOX_CELLS), ((0, 2), (1, 16)), -0.2, 0.2)), 0.05, 0.5)
    b_boxes = jnp.clip(jnp.exp(math.log(2.0) - 2.3025851 * jax.random.uniform(keys[2], (LAYERS, MEMBERS * BOXES_DEV, BOX_CELLS), jnp.float32) ** block_levels(keys[2], (LAYERS, MEMBERS * BOXES_DEV, BOX_CELLS), ((0, 2), (1, 16)), -0.2, 0.2)), 0.2, 2.0)
    new_place = draw_new_place(jax.random.fold_in(keys[4], 71), 0)
    return {"rhs_boxes": rhs_boxes, "a_boxes": a_boxes, "b_boxes": b_boxes, "new_place": new_place}


def stencil_sum(padded, across_x, across_y, across_z):
    summed = across_x[:-1] * padded[:-2, 1:-1, 1:-1] + across_x[1:] * padded[2:, 1:-1, 1:-1]
    summed = summed + across_y[:, :-1] * padded[1:-1, :-2, 1:-1] + across_y[:, 1:] * padded[1:-1, 2:, 1:-1]
    summed = summed + across_z[:, :, :-1] * padded[1:-1, 1:-1, :-2] + across_z[:, :, 1:] * padded[1:-1, 1:-1, 2:]
    return summed


def face_total(across_x, across_y, across_z):
    return across_x[:-1] + across_x[1:] + across_y[:, :-1] + across_y[:, 1:] + across_z[:, :, :-1] + across_z[:, :, 1:]


def checker(extent):
    return (lax.broadcasted_iota(jnp.int32, extent, 0) + lax.broadcasted_iota(jnp.int32, extent, 1) + lax.broadcasted_iota(jnp.int32, extent, 2)) % 2


def red_black(solution, source, coeffs, sweeps):
    diagonal, across_x, across_y, across_z, weight = coeffs
    colour = checker(solution.shape)
    for repeat in range(sweeps):
        for current in (0, 1):
            padded = jnp.pad(solution, 1)
            updated = (source + weight * stencil_sum(padded, across_x, across_y, across_z)) / diagonal
            solution = jnp.where(colour == current, updated, solution)
    return solution


def misfit(solution, source, coeffs):
    diagonal, across_x, across_y, across_z, weight = coeffs
    padded = jnp.pad(solution, 1)
    return source - (diagonal * solution - weight * stencil_sum(padded, across_x, across_y, across_z))


def restrict(values):
    size_x, size_y, size_z = values.shape
    return values.reshape(size_x // 2, 2, size_y // 2, 2, size_z // 2, 2).mean(axis=(1, 3, 5))


def coarse_faces(across_x, across_y, across_z):
    size_x, size_y, size_z = across_x.shape[0] - 1, across_x.shape[1], across_x.shape[2]
    coarse_x = across_x[0::2].reshape(size_x // 2 + 1, size_y // 2, 2, size_z // 2, 2).mean(axis=(2, 4))
    coarse_y = across_y[:, 0::2].reshape(size_x // 2, 2, size_y // 2 + 1, size_z // 2, 2).mean(axis=(1, 4))
    coarse_z = across_z[:, :, 0::2].reshape(size_x // 2, 2, size_y // 2, 2, size_z // 2 + 1).mean(axis=(1, 3))
    return coarse_x, coarse_y, coarse_z


def prolong(values):
    size_x, size_y, size_z = values.shape
    spread = jnp.broadcast_to(values[:, None, :, None, :, None], (size_x, 2, size_y, 2, size_z, 2))
    return spread.reshape(2 * size_x, 2 * size_y, 2 * size_z)


def place(values, new_place):
    layer_ids = jnp.arange(LAYERS, dtype=jnp.int32)[:, None]
    placed = jnp.zeros_like(values).at[layer_ids, new_place].set(values)
    shaped = placed.reshape(LAYERS, N_GX, N_GY, 2, BOXES_Z, BOX_EDGE, BOX_EDGE, BOX_EDGE)
    return shaped.transpose(1, 3, 5, 2, 6, 0, 4, 7).reshape(NX, NY, NZ)


def reference(rhs_boxes, a_boxes, b_boxes, new_place):
    rhs = place(rhs_boxes, new_place)
    acoef = place(a_boxes, new_place)
    bcoef = place(b_boxes, new_place)
    padded_b = jnp.pad(bcoef, 1)
    across_x = 0.5 * (padded_b[1:, 1:-1, 1:-1] + padded_b[:-1, 1:-1, 1:-1])
    across_y = 0.5 * (padded_b[1:-1, 1:, 1:-1] + padded_b[1:-1, :-1, 1:-1])
    across_z = 0.5 * (padded_b[1:-1, 1:-1, 1:] + padded_b[1:-1, 1:-1, :-1])
    fine_level = (acoef + 1.0 * face_total(across_x, across_y, across_z), across_x, across_y, across_z, 1.0)
    smoothed = red_black(jnp.zeros_like(rhs), rhs, fine_level, SWEEPS)
    coarse_rhs = restrict(misfit(smoothed, rhs, fine_level))
    coarse_x, coarse_y, coarse_z = coarse_faces(across_x, across_y, across_z)
    coarse = (restrict(acoef) + 0.25 * face_total(coarse_x, coarse_y, coarse_z), coarse_x, coarse_y, coarse_z, 0.25)
    correction = red_black(jnp.zeros_like(coarse_rhs), coarse_rhs, coarse, COARSE_SWEEPS)
    solution = red_black(smoothed + prolong(correction), rhs, fine_level, SWEEPS)
    return solution, misfit(solution, rhs, fine_level)
```

```python
import functools

import jax
import jax.numpy as jnp
from jax import lax
from jax.experimental import pallas as pl
from jax.experimental.pallas import tpu as pltpu
from jax.sharding import PartitionSpec as P

MESH = pl.DeviceIdType.MESH
NX, NY, NZ = 64, 32, 64
LANES = 128
COARSE_HALVES = 8
EXCHANGES = 13
F32 = jnp.float32


def lane_ids():
    return lax.broadcasted_iota(jnp.int32, (NY, LANES), 1)


def row_ids():
    return lax.broadcasted_iota(jnp.int32, (NY, LANES), 0)


def pair_z(v):
    return v + jnp.where(lane_ids() % 2 == 0, pltpu.roll(v, LANES - 1, 1), pltpu.roll(v, 1, 1))


def pair_y(v):
    return v + jnp.where(row_ids() % 2 == 0, pltpu.roll(v, NY - 1, 0), pltpu.roll(v, 1, 0))


def even_y(v):
    return jnp.where(row_ids() % 2 == 0, v, pltpu.roll(v, 1, 0))


def odd_y(v):
    return jnp.where(row_ids() % 2 == 1, v, pltpu.roll(v, NY - 1, 0))


def even_z(v):
    return jnp.where(lane_ids() % 2 == 0, v, pltpu.roll(v, 1, 1))


def odd_z(v):
    return jnp.where(lane_ids() % 2 == 1, v, pltpu.roll(v, LANES - 1, 1))


def kernel(
    sizes,
    place_ref, rhs_in, a_in, b_in,
    sol_out, res_out,
    got_place, inv_vmem, inv_smem, got_b, got_a, got_rhs, sorted_, final,
    bv, rh, ac, dg, rd, fx, fyl, fyh, fzl, fzh, v,
    cc, cf, crd, cfx, cfyl, cfyh, cfzl, cfzh,
    hx, hy, hz, ys, zs,
    place_send, place_recv, send1, recv1, send2, recv2, inv_sem, halo_send, halo_recv,
):
    n_gx, n_gy, n_gz = sizes
    members = n_gx * n_gy
    rows = 256 // members
    slabs = rows // 8
    gx, gy, gz = lax.axis_index("gx"), lax.axis_index("gy"), lax.axis_index("gz")
    me = gx * n_gy + gy
    got = (got_b, got_a, got_rhs)

    def member(t):
        return (t // n_gy, t % n_gy, gz)

    @pl.loop(0, EXCHANGES)
    def _(e):
        for side in range(2):
            hx[e, side] = jnp.zeros((NY, LANES), F32)
            hy[e, side] = jnp.zeros((NX, LANES), F32)
            hz[e, side] = jnp.zeros((NY, LANES), F32)

    barrier = pltpu.get_barrier_semaphore()

    @pl.loop(1, members)
    def _(k):
        pl.semaphore_signal(barrier, inc=1, device_id=member((me + k) % members), device_id_type=MESH)

    @pl.when(gz > 0)
    def _():
        pl.semaphore_signal(barrier, inc=1, device_id=(gx, gy, gz - 1), device_id_type=MESH)

    @pl.when(gz < n_gz - 1)
    def _():
        pl.semaphore_signal(barrier, inc=1, device_id=(gx, gy, gz + 1), device_id_type=MESH)

    pl.semaphore_wait(
        barrier, members - 1 + (gz > 0).astype(jnp.int32) + (gz < n_gz - 1).astype(jnp.int32)
    )

    def place_copy(peer, k, slot):
        return pltpu.make_async_remote_copy(
            src_ref=place_ref, dst_ref=got_place.at[slot],
            send_sem=place_send.at[k], recv_sem=place_recv.at[slot],
            device_id=member(peer), device_id_type=MESH,
        )

    def copy1(f, peer, k, slot):
        return pltpu.make_async_remote_copy(
            src_ref=(b_in, a_in, rhs_in)[f].at[pl.ds(pl.multiple_of(peer * 4 * rows, 8), 4 * rows)],
            dst_ref=got[f].at[slot],
            send_sem=send1.at[f, k], recv_sem=recv1.at[f, slot],
            device_id=member(peer), device_id_type=MESH,
        )

    def copy2(f, peer, k, slot):
        return pltpu.make_async_remote_copy(
            src_ref=sorted_.at[f, peer], dst_ref=final.at[f, slot],
            send_sem=send2.at[f, k], recv_sem=recv2.at[f, slot],
            device_id=member(peer), device_id_type=MESH,
        )

    @pl.loop(1, members)
    def _(k):
        place_copy((me + k) % members, k, me).start()

    for f in range(3):
        @pl.loop(1, members)
        def _(k):
            copy1(f, (me + k) % members, k, me).start()

    got_place[me] = place_ref[...]
    for f in range(3):
        got[f][me] = (b_in, a_in, rhs_in)[f][pl.ds(pl.multiple_of(me * 4 * rows, 8), 4 * rows), :]

    @pl.loop(1, members)
    def _(k):
        place_copy((me + k) % members, k, (me + k) % members).wait_recv()

    lane8 = lax.broadcasted_iota(jnp.int32, (8, LANES), 1)
    row8 = lax.broadcasted_iota(jnp.int32, (8, LANES), 0)

    def find(src, total):
        here = (got_place[src] == lane8) & (row8 < 4)
        return jnp.maximum(total, jnp.where(here, src * 4 + row8, 0))

    owner = lax.fori_loop(0, members, find, jnp.zeros((8, LANES), jnp.int32))
    for shift in (4, 2, 1):
        owner = jnp.maximum(owner, pltpu.roll(owner, shift, 0))
    inv_vmem[...] = owner
    inv_copy = pltpu.make_async_copy(inv_vmem, inv_smem, inv_sem)
    inv_copy.start()
    inv_copy.wait()

    def forward(f):
        @pl.loop(1, members)
        def _(k):
            copy1(f, (me + k) % members, k, (me + k) % members).wait_recv()

        def pick(t, q):
            index = inv_smem[0, t * 4 + q]
            return got[f][index >> 2, pl.ds(index & 3, rows, stride=4), :]

        @pl.loop(1, members)
        def _(k):
            t = (me + k) % members
            for q in range(4):
                sorted_[f, t, q * rows:(q + 1) * rows, :] = pick(t, q)
            copy2(f, t, k, me).start()

        for q in range(4):
            final[f, me, q * rows:(q + 1) * rows, :] = pick(me, q)

    def unpack(f, out, first):
        @pl.loop(1, members)
        def _(k):
            copy2(f, (me + k) % members, k, (me + k) % members).wait_recv()

        @pl.loop(0, members)
        def _(j):
            for qx in range(2):
                for slab in range(slabs):
                    low = qx * 2 * rows + slab * 8
                    t0 = final[f, j, low:low + 8, :]
                    t1 = final[f, j, low + rows:low + rows + 8, :]
                    x = qx * 32 + j * slabs + slab
                    for yr in range(4):
                        r0 = pltpu.roll(t0, (LANES - 32 * yr) % LANES, 1)
                        r1 = pltpu.roll(t1, (LANES + 32 - 32 * yr) % LANES, 1)
                        out[x + first, pl.ds(yr, 8, stride=4), :] = jnp.where(lane8 < 32, r0, r1)

    def exchange(e, field, planes):
        for act in ("start", "wait"):
            for axis in range(3):
                for side in range(2):
                    d = axis * 2 + side
                    place, count = ((gx, n_gx), (gy, n_gy), (gz, n_gz))[axis]
                    there = place > 0 if side == 0 else place < count - 1
                    other = [gx, gy, gz]
                    other[axis] = place + (2 * side - 1)
                    if axis == 0:
                        src, dst = field.at[1 if side == 0 else planes], hx
                        to, mine = dst.at[e, 1 - side], dst.at[e, side]
                    elif axis == 1:
                        src = ys.at[side, pl.ds(0, planes)]
                        to, mine = hy.at[e, 1 - side, pl.ds(0, planes)], hy.at[e, side, pl.ds(0, planes)]
                    else:
                        src, to, mine = zs, hz.at[e, 1 - side], hz.at[e, side]

                    @pl.when(there)
                    def _():
                        out = pltpu.make_async_remote_copy(
                            src_ref=src, dst_ref=to, send_sem=halo_send.at[d],
                            recv_sem=halo_recv.at[e, axis * 2 + 1 - side],
                            device_id=tuple(other), device_id_type=MESH,
                        )
                        if act == "start":
                            out.start()
                        else:
                            out.wait_send()
                            pltpu.make_async_remote_copy(
                                src_ref=src, dst_ref=mine, send_sem=halo_send.at[d],
                                recv_sem=halo_recv.at[e, d],
                                device_id=tuple(other), device_id_type=MESH,
                            ).wait_recv()
        field[0] = hx[e, 0]
        field[planes + 1] = hx[e, 1]

    def stage(n, x, st, packed):
        ys[0, pl.ds(x, 1), :] = n[0:1, :]
        ys[1, pl.ds(x, 1), :] = n[NY - 1:NY, :]
        group = lane_ids() // st
        top = pltpu.roll(n, (x * st + LANES - (NZ - st)) % LANES, 1)
        bottom = pltpu.roll(n, (x * st + 64) % LANES, 1)
        return jnp.where(group == x, top, jnp.where(group == x + 64 // st, bottom, packed))

    def beside(field, e, x, st):
        c = field[x + 1]
        lane, row = lane_ids(), row_ids()
        yl = jnp.where(row < st, hy[e, 0, pl.ds(x, 1), :], pltpu.roll(c, st, 0))
        yh = jnp.where(row >= NY - st, hy[e, 1, pl.ds(x, 1), :], pltpu.roll(c, NY - st, 0))
        low = pltpu.roll(hz[e, 0], (2 * LANES - st - x * st) % LANES, 1)
        high = pltpu.roll(hz[e, 1], (LANES - x * st) % LANES, 1)
        w = jnp.where(lane >= LANES - st, low, jnp.where(lane >= NZ, high, c))
        return c, field[x], field[x + 2], yl, yh, pltpu.roll(w, st, 1), pltpu.roll(w, LANES - st, 1)

    def fine_nb(e, x):
        c, xl, xh, yl, yh, zl, zh = beside(v, e, x, 1)
        return c, (
            (fx[x] * xl + fx[x + 1] * xh) + (fyl[x] * yl + fyh[x] * yh) + (fzl[x] * zl + fzh[x] * zh)
        )

    def coarse_nb(e, x):
        c, xl, xh, yl, yh, zl, zh = beside(cc, e, x, 2)
        return c, (
            (cfx[x] * xl + cfx[x + 1] * xh) + (cfyl[x] * yl + cfyh[x] * yh) + (cfzl[x] * zl + cfzh[x] * zh)
        )

    def sweep(planes, body):
        zs[...] = lax.fori_loop(0, planes, body, jnp.zeros((NY, LANES), F32))

    def is_colour(x, st, colour):
        return (row_ids() // st + lane_ids() // st + x + colour) % 2 == 0

    forward(0)
    forward(1)
    unpack(0, bv, 1)
    sweep(NX, lambda x, packed: stage(bv[x + 1], x, 1, packed))
    exchange(0, bv, NX)
    forward(2)

    @pl.loop(0, NX)
    def _(x):
        c, xl, xh, yl, yh, zl, zh = beside(bv, 0, x, 1)
        fx[x] = 0.5 * (c + xl)
        fyl[x] = 0.5 * (c + yl)
        fyh[x] = 0.5 * (c + yh)
        fzl[x] = 0.5 * (c + zl)
        fzh[x] = 0.5 * (c + zh)

    fx[NX] = 0.5 * (bv[NX] + bv[NX + 1])

    unpack(1, ac, 0)

    @pl.loop(0, NX // 2)
    def _(i):
        x = 2 * i
        for o in range(2):
            d = ac[x + o] + (
                (fx[x + o] + fx[x + o + 1]) + (fyl[x + o] + fyh[x + o]) + (fzl[x + o] + fzh[x + o])
            )
            dg[x + o] = d
            rd[x + o] = 1.0 / d
        s = 0.0625
        wxl = s * pair_z(pair_y(fx[x]))
        wxh = s * pair_z(pair_y(fx[x + 2]))
        wyl = s * pair_z(even_y(fyl[x] + fyl[x + 1]))
        wyh = s * pair_z(odd_y(fyh[x] + fyh[x + 1]))
        wzl = s * pair_y(even_z(fzl[x] + fzl[x + 1]))
        wzh = s * pair_y(odd_z(fzh[x] + fzh[x + 1]))
        cfx[i] = wxl
        cfx[i + 1] = wxh
        cfyl[i] = wyl
        cfyh[i] = wyh
        cfzl[i] = wzl
        cfzh[i] = wzh
        ca = 0.125 * pair_z(pair_y(ac[x] + ac[x + 1]))
        crd[i] = 1.0 / (ca + ((wxl + wxh) + (wyl + wyh) + (wzl + wzh)))

    unpack(2, rh, 0)

    def first_red(x, packed):
        n = jnp.where(is_colour(x, 1, 0), rh[x] * rd[x], 0.0)
        v[x + 1] = n
        return stage(n, x, 1, packed)

    def half(e, colour, staged):
        def step(x, packed):
            c, nb = fine_nb(e, x)
            n = jnp.where(is_colour(x, 1, colour), (rh[x] + nb) * rd[x], c)
            v[x + 1] = n
            return stage(n, x, 1, packed)

        sweep(NX, step)

    sweep(NX, first_red)
    exchange(1, v, NX)
    half(1, 1, True)
    exchange(2, v, NX)

    def first_coarse(i, packed):
        total = None
        for o in range(2):
            c, nb = fine_nb(2, 2 * i + o)
            r = rh[2 * i + o] - (dg[2 * i + o] * c - nb)
            total = r if total is None else total + r
        f = 0.125 * pair_z(pair_y(total))
        cf[i] = f
        n = jnp.where(is_colour(i, 2, 0), f * crd[i], 0.0)
        cc[i + 1] = n
        return stage(n, i, 2, packed)

    sweep(NX // 2, first_coarse)

    @pl.loop(1, COARSE_HALVES)
    def _(h):
        e = 2 + h
        exchange(e, cc, NX // 2)

        def step(i, packed):
            c, nb = coarse_nb(e, i)
            n = jnp.where(is_colour(i, 2, h), (cf[i] + nb) * crd[i], c)
            cc[i + 1] = n
            return stage(n, i, 2, packed)

        sweep(NX // 2, step)

    def correct(i, packed):
        c = cc[i + 1]
        for o in range(2):
            n = v[2 * i + o + 1] + c
            v[2 * i + o + 1] = n
            packed = stage(n, 2 * i + o, 1, packed)
        return packed

    sweep(NX // 2, correct)
    exchange(10, v, NX)
    half(10, 0, True)
    exchange(11, v, NX)
    half(11, 1, True)
    exchange(12, v, NX)

    @pl.loop(0, NX)
    def _(x):
        c, nb = fine_nb(12, x)
        sol_out[x] = c[:, :NZ]
        res_out[x] = (rh[x] - (dg[x] * c - nb))[:, :NZ]

    @pl.loop(1, members)
    def _(k):
        peer = (me + k) % members
        place_copy(peer, k, me).wait_send()
        for f in range(3):
            copy1(f, peer, k, me).wait_send()
            copy2(f, peer, k, me).wait_send()


def solution(mesh):
    sizes = (mesh.shape["gx"], mesh.shape["gy"], mesh.shape["gz"])
    members = sizes[0] * sizes[1]
    rows = 256 // members

    def rows128(boxes):
        return boxes[0].reshape(4, 256, LANES).transpose(1, 0, 2).reshape(1024, LANES)

    def body(rhs_boxes, a_boxes, b_boxes, new_place):
        spot = jnp.where(jnp.arange(8)[:, None] < 4, jnp.tile(new_place[0], 2)[:, None], -1)
        spot = jnp.broadcast_to(spot, (8, LANES)).astype(jnp.int32)
        fine = pltpu.VMEM((NX, NY, LANES), F32)
        coarse = pltpu.VMEM((NX // 2, NY, LANES), F32)
        box = pltpu.VMEM((members, 4 * rows, LANES), F32)
        boxes = pltpu.VMEM((3, members, 4 * rows, LANES), F32)
        dma = pltpu.SemaphoreType.DMA
        return pl.pallas_call(
            functools.partial(kernel, sizes),
            out_shape=[jax.ShapeDtypeStruct((NX, NY, NZ), F32)] * 2,
            in_specs=[pl.BlockSpec(memory_space=pltpu.VMEM)] * 4,
            out_specs=[pl.BlockSpec(memory_space=pltpu.VMEM)] * 2,
            scratch_shapes=[
                pltpu.VMEM((members, 8, LANES), jnp.int32),
                pltpu.VMEM((8, LANES), jnp.int32),
                pltpu.SMEM((8, LANES), jnp.int32),
                box, box, box, boxes, boxes,
                pltpu.VMEM((NX + 2, NY, LANES), F32),
                fine, fine, fine, fine,
                pltpu.VMEM((NX + 1, NY, LANES), F32),
                fine, fine, fine, fine,
                pltpu.VMEM((NX + 2, NY, LANES), F32),
                pltpu.VMEM((NX // 2 + 2, NY, LANES), F32),
                coarse, coarse,
                pltpu.VMEM((NX // 2 + 1, NY, LANES), F32),
                coarse, coarse, coarse, coarse,
                pltpu.VMEM((EXCHANGES, 2, NY, LANES), F32),
                pltpu.VMEM((EXCHANGES, 2, NX, LANES), F32),
                pltpu.VMEM((EXCHANGES, 2, NY, LANES), F32),
                pltpu.VMEM((2, NX, LANES), F32),
                pltpu.VMEM((NY, LANES), F32),
                dma((members,)), dma((members,)),
                dma((3, members)), dma((3, members)),
                dma((3, members)), dma((3, members)),
                dma,
                dma((6,)), dma((EXCHANGES, 6)),
            ],
            compiler_params=pltpu.CompilerParams(
                collective_id=0, has_side_effects=True, vmem_limit_bytes=48 * 1024 * 1024
            ),
        )(spot, rows128(rhs_boxes), rows128(a_boxes), rows128(b_boxes))

    return jax.shard_map(
        body,
        mesh=mesh,
        in_specs=(
            P("gz", ("gx", "gy"), None),
            P("gz", ("gx", "gy"), None),
            P("gz", ("gx", "gy"), None),
            P("gz", ("gx", "gy")),
        ),
        out_specs=(P("gx", "gy", "gz"), P("gx", "gy", "gz")),
        check_vma=False,
    )
```

```python
import functools

import jax
import jax.numpy as jnp
from jax import lax
from jax.experimental import pallas as pl
from jax.experimental.pallas import tpu as pltpu
from jax.sharding import PartitionSpec as P

MESH = pl.DeviceIdType.MESH
NX, NY, NZ = 64, 32, 64
LANES = 128
COARSE_HALVES = 8
EXCHANGES = 13
GROUP = 4
F32 = jnp.float32


def lane_ids():
    return lax.broadcasted_iota(jnp.int32, (NY, LANES), 1)


def row_ids():
    return lax.broadcasted_iota(jnp.int32, (NY, LANES), 0)


def pair_z(v):
    return v + jnp.where(lane_ids() % 2 == 0, pltpu.roll(v, LANES - 1, 1), pltpu.roll(v, 1, 1))


def pair_y(v):
    return v + jnp.where(row_ids() % 2 == 0, pltpu.roll(v, NY - 1, 0), pltpu.roll(v, 1, 0))


def even_y(v):
    return jnp.where(row_ids() % 2 == 0, v, pltpu.roll(v, 1, 0))


def odd_y(v):
    return jnp.where(row_ids() % 2 == 1, v, pltpu.roll(v, NY - 1, 0))


def even_z(v):
    return jnp.where(lane_ids() % 2 == 0, v, pltpu.roll(v, 1, 1))


def odd_z(v):
    return jnp.where(lane_ids() % 2 == 1, v, pltpu.roll(v, LANES - 1, 1))


def kernel(
    sizes,
    place_ref, rhs_in, a_in, b_in,
    sol_out, res_out,
    got_place, inv_vmem, inv_smem, got_b, got_a, got_rhs, sorted_, final,
    bv, rh, ac, dg, rd, fx, fyl, fyh, fzl, fzh, v,
    cc, cf, crd, cfx, cfyl, cfyh, cfzl, cfzh,
    hx, hy, hz, ys, zs,
    place_send, place_recv, send1, recv1, send2, recv2, inv_sem, halo_send, halo_recv,
):
    n_gx, n_gy, n_gz = sizes
    members = n_gx * n_gy
    rows = 256 // members
    slabs = rows // 8
    gx, gy, gz = lax.axis_index("gx"), lax.axis_index("gy"), lax.axis_index("gz")
    me = gx * n_gy + gy
    got = (got_b, got_a, got_rhs)

    def member(t):
        return (t // n_gy, t % n_gy, gz)

    @pl.loop(0, EXCHANGES)
    def _(e):
        for side in range(2):
            hx[e, side] = jnp.zeros((NY, LANES), F32)
            hy[e, side] = jnp.zeros((NX, LANES), F32)
            hz[e, side] = jnp.zeros((2, NY, LANES), F32)

    barrier = pltpu.get_barrier_semaphore()

    @pl.loop(1, members)
    def _(k):
        pl.semaphore_signal(barrier, inc=1, device_id=member((me + k) % members), device_id_type=MESH)

    @pl.when(gz > 0)
    def _():
        pl.semaphore_signal(barrier, inc=1, device_id=(gx, gy, gz - 1), device_id_type=MESH)

    @pl.when(gz < n_gz - 1)
    def _():
        pl.semaphore_signal(barrier, inc=1, device_id=(gx, gy, gz + 1), device_id_type=MESH)

    pl.semaphore_wait(
        barrier, members - 1 + (gz > 0).astype(jnp.int32) + (gz < n_gz - 1).astype(jnp.int32)
    )

    def place_copy(peer, k, slot):
        return pltpu.make_async_remote_copy(
            src_ref=place_ref, dst_ref=got_place.at[slot],
            send_sem=place_send.at[k], recv_sem=place_recv.at[slot],
            device_id=member(peer), device_id_type=MESH,
        )

    def copy1(f, peer, k, slot):
        return pltpu.make_async_remote_copy(
            src_ref=(b_in, a_in, rhs_in)[f].at[pl.ds(pl.multiple_of(peer * 4 * rows, 8), 4 * rows)],
            dst_ref=got[f].at[slot],
            send_sem=send1.at[f, k], recv_sem=recv1.at[f, slot],
            device_id=member(peer), device_id_type=MESH,
        )

    def copy2(f, peer, k, slot):
        return pltpu.make_async_remote_copy(
            src_ref=sorted_.at[f, peer], dst_ref=final.at[f, slot],
            send_sem=send2.at[f, k], recv_sem=recv2.at[f, slot],
            device_id=member(peer), device_id_type=MESH,
        )

    @pl.loop(1, members)
    def _(k):
        place_copy((me + k) % members, k, me).start()

    for f in range(3):
        @pl.loop(1, members)
        def _(k):
            copy1(f, (me + k) % members, k, me).start()

    got_place[me] = place_ref[...]
    for f in range(3):
        got[f][me] = (b_in, a_in, rhs_in)[f][pl.ds(pl.multiple_of(me * 4 * rows, 8), 4 * rows), :]

    @pl.loop(1, members)
    def _(k):
        place_copy((me + k) % members, k, (me + k) % members).wait_recv()

    lane8 = lax.broadcasted_iota(jnp.int32, (8, LANES), 1)
    row8 = lax.broadcasted_iota(jnp.int32, (8, LANES), 0)

    def find(src, total):
        here = (got_place[src] == lane8) & (row8 < 4)
        return jnp.maximum(total, jnp.where(here, src * 4 + row8, 0))

    owner = lax.fori_loop(0, members, find, jnp.zeros((8, LANES), jnp.int32))
    for shift in (4, 2, 1):
        owner = jnp.maximum(owner, pltpu.roll(owner, shift, 0))
    inv_vmem[...] = owner
    inv_copy = pltpu.make_async_copy(inv_vmem, inv_smem, inv_sem)
    inv_copy.start()
    inv_copy.wait()

    def forward(f):
        @pl.loop(1, members)
        def _(k):
            copy1(f, (me + k) % members, k, (me + k) % members).wait_recv()

        def pick(t, q):
            index = inv_smem[0, t * 4 + q]
            return got[f][index >> 2, pl.ds(index & 3, rows, stride=4), :]

        @pl.loop(1, members)
        def _(k):
            t = (me + k) % members
            for q in range(4):
                sorted_[f, t, q * rows:(q + 1) * rows, :] = pick(t, q)
            copy2(f, t, k, me).start()

        for q in range(4):
            final[f, me, q * rows:(q + 1) * rows, :] = pick(me, q)

    def unpack(f, out, first):
        @pl.loop(1, members)
        def _(k):
            copy2(f, (me + k) % members, k, (me + k) % members).wait_recv()

        @pl.loop(0, members)
        def _(j):
            for qx in range(2):
                for slab in range(slabs):
                    low = qx * 2 * rows + slab * 8
                    t0 = final[f, j, low:low + 8, :]
                    t1 = final[f, j, low + rows:low + rows + 8, :]
                    x = qx * 32 + j * slabs + slab
                    for yr in range(4):
                        r0 = pltpu.roll(t0, (LANES - 32 * yr) % LANES, 1)
                        r1 = pltpu.roll(t1, (LANES + 32 - 32 * yr) % LANES, 1)
                        out[x + first, pl.ds(yr, 8, stride=4), :] = jnp.where(lane8 < 32, r0, r1)

    def exchange(e, field, planes):
        for act in ("start", "wait"):
            for axis in range(3):
                for side in range(2):
                    d = axis * 2 + side
                    place, count = ((gx, n_gx), (gy, n_gy), (gz, n_gz))[axis]
                    there = place > 0 if side == 0 else place < count - 1
                    other = [gx, gy, gz]
                    other[axis] = place + (2 * side - 1)
                    if axis == 0:
                        src, dst = field.at[1 if side == 0 else planes], hx
                        to, mine = dst.at[e, 1 - side], dst.at[e, side]
                    elif axis == 1:
                        src = ys.at[side, pl.ds(0, planes)]
                        to, mine = hy.at[e, 1 - side, pl.ds(0, planes)], hy.at[e, side, pl.ds(0, planes)]
                    else:
                        src, to, mine = zs, hz.at[e, 1 - side], hz.at[e, side]

                    @pl.when(there)
                    def _():
                        out = pltpu.make_async_remote_copy(
                            src_ref=src, dst_ref=to, send_sem=halo_send.at[d],
                            recv_sem=halo_recv.at[e, axis * 2 + 1 - side],
                            device_id=tuple(other), device_id_type=MESH,
                        )
                        if act == "start":
                            out.start()
                        else:
                            out.wait_send()
                            pltpu.make_async_remote_copy(
                                src_ref=src, dst_ref=mine, send_sem=halo_send.at[d],
                                recv_sem=halo_recv.at[e, d],
                                device_id=tuple(other), device_id_type=MESH,
                            ).wait_recv()
        field[0] = hx[e, 0]
        field[planes + 1] = hx[e, 1]

    def level_pass(planes, st, body, staged=True, field=None, e=None):
        half_planes = planes // 2
        spot = ((lane_ids() + st) % LANES) // st
        lane, row = lane_ids(), row_ids()
        for h in range(2):
            if e is not None:
                beyond = jnp.where(spot < 48 // st, hz[e, 0, h], hz[e, 1, h])

            def step(g, packed):
                near = [g * GROUP + i for i in range(GROUP)]
                xs = [h * half_planes + n for n in near]
                hoods = [None] * GROUP
                if e is not None:
                    loaded = [field[xs[0] + i] for i in range(GROUP + 2)]
                    hoods = []
                    for i in range(GROUP):
                        c = loaded[i + 1]
                        yl = jnp.where(row < st, hy[e, 0, pl.ds(xs[i], 1), :], pltpu.roll(c, st, 0))
                        yh = jnp.where(
                            row >= NY - st, hy[e, 1, pl.ds(xs[i], 1), :], pltpu.roll(c, NY - st, 0)
                        )
                        w = jnp.where(
                            lane >= NZ, pltpu.roll(beyond, (LANES - near[i] * st) % LANES, 1), c
                        )
                        zl, zh = pltpu.roll(w, st, 1), pltpu.roll(w, LANES - st, 1)
                        hoods.append((c, loaded[i], loaded[i + 2], yl, yh, zl, zh))
                results = body(xs, hoods)
                if staged:
                    for i in range(GROUP):
                        n = results[i]
                        turned = pltpu.roll(n, (near[i] * st + 64) % LANES, 1)
                        mine = (spot == near[i]) | (spot == near[i] + 64 // st + 1)
                        packed = jnp.where(mine, turned, packed)
                    for i in range(GROUP):
                        ys[0, pl.ds(xs[i], 1), :] = results[i][0:1, :]
                        ys[1, pl.ds(xs[i], 1), :] = results[i][NY - 1:NY, :]
                    return packed
                return packed

            steps = half_planes // GROUP
            if staged:
                zs[h] = lax.fori_loop(0, steps, step, jnp.zeros((NY, LANES), F32))
            else:
                lax.fori_loop(0, steps, step, 0)

    def fine_nb(x, hood):
        c, xl, xh, yl, yh, zl, zh = hood
        return c, (
            (fx[x] * xl + fx[x + 1] * xh) + (fyl[x] * yl + fyh[x] * yh) + (fzl[x] * zl + fzh[x] * zh)
        )

    def coarse_nb(x, hood):
        c, xl, xh, yl, yh, zl, zh = hood
        return c, (
            (cfx[x] * xl + cfx[x + 1] * xh) + (cfyl[x] * yl + cfyh[x] * yh) + (cfzl[x] * zl + cfzh[x] * zh)
        )

    def is_colour(x, st, colour):
        return (row_ids() // st + lane_ids() // st + x + colour) % 2 == 0

    forward(0)
    forward(1)
    unpack(0, bv, 1)
    level_pass(NX, 1, lambda xs, hoods: [bv[x + 1] for x in xs])
    exchange(0, bv, NX)
    forward(2)

    def faces(xs, hoods):
        for x, (c, xl, xh, yl, yh, zl, zh) in zip(xs, hoods):
            fx[x] = 0.5 * (c + xl)
            fyl[x] = 0.5 * (c + yl)
            fyh[x] = 0.5 * (c + yh)
            fzl[x] = 0.5 * (c + zl)
            fzh[x] = 0.5 * (c + zh)

    level_pass(NX, 1, faces, staged=False, field=bv, e=0)
    fx[NX] = 0.5 * (bv[NX] + bv[NX + 1])

    unpack(1, ac, 0)

    @pl.loop(0, NX // 2)
    def _(i):
        x = 2 * i
        for o in range(2):
            d = ac[x + o] + (
                (fx[x + o] + fx[x + o + 1]) + (fyl[x + o] + fyh[x + o]) + (fzl[x + o] + fzh[x + o])
            )
            dg[x + o] = d
            rd[x + o] = 1.0 / d
        s = 0.0625
        wxl = s * pair_z(pair_y(fx[x]))
        wxh = s * pair_z(pair_y(fx[x + 2]))
        wyl = s * pair_z(even_y(fyl[x] + fyl[x + 1]))
        wyh = s * pair_z(odd_y(fyh[x] + fyh[x + 1]))
        wzl = s * pair_y(even_z(fzl[x] + fzl[x + 1]))
        wzh = s * pair_y(odd_z(fzh[x] + fzh[x + 1]))
        cfx[i] = wxl
        cfx[i + 1] = wxh
        cfyl[i] = wyl
        cfyh[i] = wyh
        cfzl[i] = wzl
        cfzh[i] = wzh
        ca = 0.125 * pair_z(pair_y(ac[x] + ac[x + 1]))
        crd[i] = 1.0 / (ca + ((wxl + wxh) + (wyl + wyh) + (wzl + wzh)))

    unpack(2, rh, 0)

    def store(field, xs, values):
        for x, n in zip(xs, values):
            field[x + 1] = n
        return values

    def first_red(xs, hoods):
        return store(v, xs, [jnp.where(is_colour(x, 1, 0), rh[x] * rd[x], 0.0) for x in xs])

    def half(e, colour):
        def update(xs, hoods):
            values = []
            for x, hood in zip(xs, hoods):
                c, nb = fine_nb(x, hood)
                values.append(jnp.where(is_colour(x, 1, colour), (rh[x] + nb) * rd[x], c))
            return store(v, xs, values)

        level_pass(NX, 1, update, field=v, e=e)

    level_pass(NX, 1, first_red)
    exchange(1, v, NX)
    half(1, 1)
    exchange(2, v, NX)

    def restrict(xs, hoods):
        for p in range(0, GROUP, 2):
            total = None
            for x, hood in zip(xs[p:p + 2], hoods[p:p + 2]):
                c, nb = fine_nb(x, hood)
                r = rh[x] - (dg[x] * c - nb)
                total = r if total is None else total + r
            cf[xs[p] // 2] = 0.125 * pair_z(pair_y(total))

    level_pass(NX, 1, restrict, staged=False, field=v, e=2)

    def first_coarse(xs, hoods):
        return store(cc, xs, [jnp.where(is_colour(x, 2, 0), cf[x] * crd[x], 0.0) for x in xs])

    level_pass(NX // 2, 2, first_coarse)

    @pl.loop(1, COARSE_HALVES)
    def _(h):
        e = 2 + h
        exchange(e, cc, NX // 2)

        def update(xs, hoods):
            values = []
            for x, hood in zip(xs, hoods):
                c, nb = coarse_nb(x, hood)
                values.append(jnp.where(is_colour(x, 2, h), (cf[x] + nb) * crd[x], c))
            return store(cc, xs, values)

        level_pass(NX // 2, 2, update, field=cc, e=e)

    def correct(xs, hoods):
        coarse = [cc[xs[p] // 2 + 1] for p in range(0, GROUP, 2)]
        return store(v, xs, [v[x + 1] + coarse[i // 2] for i, x in enumerate(xs)])

    level_pass(NX, 1, correct)
    exchange(10, v, NX)
    half(10, 0)
    exchange(11, v, NX)
    half(11, 1)
    exchange(12, v, NX)

    def finish(xs, hoods):
        for x, hood in zip(xs, hoods):
            c, nb = fine_nb(x, hood)
            sol_out[x] = c[:, :NZ]
            res_out[x] = (rh[x] - (dg[x] * c - nb))[:, :NZ]

    level_pass(NX, 1, finish, staged=False, field=v, e=12)

    @pl.loop(1, members)
    def _(k):
        peer = (me + k) % members
        place_copy(peer, k, me).wait_send()
        for f in range(3):
            copy1(f, peer, k, me).wait_send()
            copy2(f, peer, k, me).wait_send()


def solution(mesh):
    sizes = (mesh.shape["gx"], mesh.shape["gy"], mesh.shape["gz"])
    members = sizes[0] * sizes[1]
    rows = 256 // members

    def rows128(boxes):
        return boxes[0].reshape(4, 256, LANES).transpose(1, 0, 2).reshape(1024, LANES)

    def body(rhs_boxes, a_boxes, b_boxes, new_place):
        spot = jnp.where(jnp.arange(8)[:, None] < 4, jnp.tile(new_place[0], 2)[:, None], -1)
        spot = jnp.broadcast_to(spot, (8, LANES)).astype(jnp.int32)
        fine = pltpu.VMEM((NX, NY, LANES), F32)
        coarse = pltpu.VMEM((NX // 2, NY, LANES), F32)
        box = pltpu.VMEM((members, 4 * rows, LANES), F32)
        boxes = pltpu.VMEM((3, members, 4 * rows, LANES), F32)
        dma = pltpu.SemaphoreType.DMA
        return pl.pallas_call(
            functools.partial(kernel, sizes),
            out_shape=[jax.ShapeDtypeStruct((NX, NY, NZ), F32)] * 2,
            in_specs=[pl.BlockSpec(memory_space=pltpu.VMEM)] * 4,
            out_specs=[pl.BlockSpec(memory_space=pltpu.VMEM)] * 2,
            scratch_shapes=[
                pltpu.VMEM((members, 8, LANES), jnp.int32),
                pltpu.VMEM((8, LANES), jnp.int32),
                pltpu.SMEM((8, LANES), jnp.int32),
                box, box, box, boxes, boxes,
                pltpu.VMEM((NX + 2, NY, LANES), F32),
                fine, fine, fine, fine,
                pltpu.VMEM((NX + 1, NY, LANES), F32),
                fine, fine, fine, fine,
                pltpu.VMEM((NX + 2, NY, LANES), F32),
                pltpu.VMEM((NX // 2 + 2, NY, LANES), F32),
                coarse, coarse,
                pltpu.VMEM((NX // 2 + 1, NY, LANES), F32),
                coarse, coarse, coarse, coarse,
                pltpu.VMEM((EXCHANGES, 2, NY, LANES), F32),
                pltpu.VMEM((EXCHANGES, 2, NX, LANES), F32),
                pltpu.VMEM((EXCHANGES, 2, 2, NY, LANES), F32),
                pltpu.VMEM((2, NX, LANES), F32),
                pltpu.VMEM((2, NY, LANES), F32),
                dma((members,)), dma((members,)),
                dma((3, members)), dma((3, members)),
                dma((3, members)), dma((3, members)),
                dma,
                dma((6,)), dma((EXCHANGES, 6)),
            ],
            compiler_params=pltpu.CompilerParams(
                collective_id=0, has_side_effects=True, vmem_limit_bytes=48 * 1024 * 1024
            ),
        )(spot, rows128(rhs_boxes), rows128(a_boxes), rows128(b_boxes))

    return jax.shard_map(
        body,
        mesh=mesh,
        in_specs=(
            P("gz", ("gx", "gy"), None),
            P("gz", ("gx", "gy"), None),
            P("gz", ("gx", "gy"), None),
            P("gz", ("gx", "gy")),
        ),
        out_specs=(P("gx", "gy", "gz"), P("gx", "gy", "gz")),
        check_vma=False,
    )
```

```python
import functools

import jax
import jax.numpy as jnp
from jax import lax
from jax.experimental import pallas as pl
from jax.experimental.pallas import tpu as pltpu
from jax.sharding import PartitionSpec as P

MESH = pl.DeviceIdType.MESH
NX, NY, NZ = 64, 32, 64
PLANES = NX // 2
LANES = 128
COARSE_HALVES = 8
EXCHANGES = 13
GROUP = 4
F32 = jnp.float32


def lane_ids():
    return lax.broadcasted_iota(jnp.int32, (NY, LANES), 1)


def row_ids():
    return lax.broadcasted_iota(jnp.int32, (NY, LANES), 0)


def pair_z(v):
    return v + jnp.where(lane_ids() % 2 == 0, pltpu.roll(v, LANES - 1, 1), pltpu.roll(v, 1, 1))


def pair_y(v):
    return v + jnp.where(row_ids() % 2 == 0, pltpu.roll(v, NY - 1, 0), pltpu.roll(v, 1, 0))


def even_y(v):
    return jnp.where(row_ids() % 2 == 0, v, pltpu.roll(v, 1, 0))


def odd_y(v):
    return jnp.where(row_ids() % 2 == 1, v, pltpu.roll(v, NY - 1, 0))


def even_z(v):
    return jnp.where(lane_ids() % 2 == 0, v, pltpu.roll(v, 1, 1))


def odd_z(v):
    return jnp.where(lane_ids() % 2 == 1, v, pltpu.roll(v, LANES - 1, 1))


def kernel(
    sizes,
    place_ref, rhs_in, a_in, b_in,
    sol_out, res_out,
    got_place, inv_vmem, inv_smem, got_b, got_a, got_rhs, sorted_, final,
    bv, rh, ac, dg, rd, fx, fyl, fyh, fzl, fzh, v,
    cc, cf, crd, cfx, cfyl, cfyh, cfzl, cfzh,
    hx, hy, hz, ys, zs,
    place_send, place_recv, send1, recv1, send2, recv2, inv_sem, halo_send, halo_recv,
):
    n_gx, n_gy, n_gz = sizes
    members = n_gx * n_gy
    rows = 256 // members
    slabs = rows // 8
    gx, gy, gz = lax.axis_index("gx"), lax.axis_index("gy"), lax.axis_index("gz")
    me = gx * n_gy + gy
    got = (got_b, got_a, got_rhs)

    def member(t):
        return (t // n_gy, t % n_gy, gz)

    @pl.loop(0, EXCHANGES)
    def _(e):
        for side in range(2):
            hx[e, side] = jnp.zeros((NY, LANES), F32)
            hy[e, side] = jnp.zeros((PLANES, LANES), F32)
            hz[e, side] = jnp.zeros((NY, LANES), F32)

    barrier = pltpu.get_barrier_semaphore()

    @pl.loop(1, members)
    def _(k):
        pl.semaphore_signal(barrier, inc=1, device_id=member((me + k) % members), device_id_type=MESH)

    @pl.when(gz > 0)
    def _():
        pl.semaphore_signal(barrier, inc=1, device_id=(gx, gy, gz - 1), device_id_type=MESH)

    @pl.when(gz < n_gz - 1)
    def _():
        pl.semaphore_signal(barrier, inc=1, device_id=(gx, gy, gz + 1), device_id_type=MESH)

    pl.semaphore_wait(
        barrier, members - 1 + (gz > 0).astype(jnp.int32) + (gz < n_gz - 1).astype(jnp.int32)
    )

    def place_copy(peer, k, slot):
        return pltpu.make_async_remote_copy(
            src_ref=place_ref, dst_ref=got_place.at[slot],
            send_sem=place_send.at[k], recv_sem=place_recv.at[slot],
            device_id=member(peer), device_id_type=MESH,
        )

    def copy1(f, peer, k, slot):
        return pltpu.make_async_remote_copy(
            src_ref=(b_in, a_in, rhs_in)[f].at[pl.ds(pl.multiple_of(peer * 4 * rows, 8), 4 * rows)],
            dst_ref=got[f].at[slot],
            send_sem=send1.at[f, k], recv_sem=recv1.at[f, slot],
            device_id=member(peer), device_id_type=MESH,
        )

    def copy2(f, peer, k, slot):
        return pltpu.make_async_remote_copy(
            src_ref=sorted_.at[f, peer], dst_ref=final.at[f, slot],
            send_sem=send2.at[f, k], recv_sem=recv2.at[f, slot],
            device_id=member(peer), device_id_type=MESH,
        )

    @pl.loop(1, members)
    def _(k):
        place_copy((me + k) % members, k, me).start()

    for f in range(3):
        @pl.loop(1, members)
        def _(k):
            copy1(f, (me + k) % members, k, me).start()

    got_place[me] = place_ref[...]
    for f in range(3):
        got[f][me] = (b_in, a_in, rhs_in)[f][pl.ds(pl.multiple_of(me * 4 * rows, 8), 4 * rows), :]

    @pl.loop(1, members)
    def _(k):
        place_copy((me + k) % members, k, (me + k) % members).wait_recv()

    lane8 = lax.broadcasted_iota(jnp.int32, (8, LANES), 1)
    row8 = lax.broadcasted_iota(jnp.int32, (8, LANES), 0)

    def find(src, total):
        here = (got_place[src] == lane8) & (row8 < 4)
        return jnp.maximum(total, jnp.where(here, src * 4 + row8, 0))

    owner = lax.fori_loop(0, members, find, jnp.zeros((8, LANES), jnp.int32))
    for shift in (4, 2, 1):
        owner = jnp.maximum(owner, pltpu.roll(owner, shift, 0))
    inv_vmem[...] = owner
    inv_copy = pltpu.make_async_copy(inv_vmem, inv_smem, inv_sem)
    inv_copy.start()
    inv_copy.wait()

    def forward(f):
        @pl.loop(1, members)
        def _(k):
            copy1(f, (me + k) % members, k, (me + k) % members).wait_recv()

        def pick(t, q):
            index = inv_smem[0, t * 4 + q]
            return got[f][index >> 2, pl.ds(index & 3, rows, stride=4), :]

        @pl.loop(1, members)
        def _(k):
            t = (me + k) % members
            for q in range(4):
                sorted_[f, t, q * rows:(q + 1) * rows, :] = pick(t, q)
            copy2(f, t, k, me).start()

        for q in range(4):
            final[f, me, q * rows:(q + 1) * rows, :] = pick(me, q)

    def unpack(f, out, first):
        @pl.loop(1, members)
        def _(k):
            copy2(f, (me + k) % members, k, (me + k) % members).wait_recv()

        @pl.loop(0, members)
        def _(j):
            for slab in range(slabs):
                tiles = [final[f, j, q * rows + slab * 8:q * rows + slab * 8 + 8, :] for q in range(4)]
                for yr in range(4):
                    whole = tiles[yr]
                    for q in range(4):
                        if q != yr:
                            turned = pltpu.roll(tiles[q], (32 * (q - yr)) % LANES, 1)
                            whole = jnp.where(lane8 // 32 == q, turned, whole)
                    out[j * slabs + slab + first, pl.ds(yr, 8, stride=4), :] = whole

    def exchange(e, field, planes):
        for act in ("start", "wait"):
            for axis in range(3):
                for side in range(2):
                    d = axis * 2 + side
                    place, count = ((gx, n_gx), (gy, n_gy), (gz, n_gz))[axis]
                    there = place > 0 if side == 0 else place < count - 1
                    other = [gx, gy, gz]
                    other[axis] = place + (2 * side - 1)
                    if axis == 0:
                        src, dst = field.at[1 if side == 0 else planes], hx
                        to, mine = dst.at[e, 1 - side], dst.at[e, side]
                    elif axis == 1:
                        src = ys.at[side, pl.ds(0, planes)]
                        to, mine = hy.at[e, 1 - side, pl.ds(0, planes)], hy.at[e, side, pl.ds(0, planes)]
                    else:
                        src, to, mine = zs, hz.at[e, 1 - side], hz.at[e, side]

                    @pl.when(there)
                    def _():
                        out = pltpu.make_async_remote_copy(
                            src_ref=src, dst_ref=to, send_sem=halo_send.at[d],
                            recv_sem=halo_recv.at[e, axis * 2 + 1 - side],
                            device_id=tuple(other), device_id_type=MESH,
                        )
                        if act == "start":
                            out.start()
                        else:
                            out.wait_send()
                            pltpu.make_async_remote_copy(
                                src_ref=src, dst_ref=mine, send_sem=halo_send.at[d],
                                recv_sem=halo_recv.at[e, d],
                                device_id=tuple(other), device_id_type=MESH,
                            ).wait_recv()
        low, lane = field[1], lane_ids()
        field[0] = pltpu.roll(jnp.where(lane >= NZ, hx[e, 0], field[planes]), NZ, 1)
        field[planes + 1] = pltpu.roll(jnp.where(lane < NZ, hx[e, 1], low), NZ, 1)

    def level_pass(planes, st, body, staged=True, field=None, e=None):
        lane, row = lane_ids(), row_ids()
        spot = ((lane + st) % NZ) // (2 * st)
        if e is not None:
            beyond = jnp.where((lane // st) % 2 == 0, hz[e, 1], pltpu.roll(hz[e, 0], 2 * st, 1))

        def step(g, packed):
            xs = [g * GROUP + i for i in range(GROUP)]
            hoods = [None] * GROUP
            if e is not None:
                loaded = [field[xs[0] + i] for i in range(GROUP + 2)]
                hoods = []
                for i in range(GROUP):
                    c = loaded[i + 1]
                    yl = jnp.where(row < st, hy[e, 0, pl.ds(xs[i], 1), :], pltpu.roll(c, st, 0))
                    yh = jnp.where(row >= NY - st, hy[e, 1, pl.ds(xs[i], 1), :], pltpu.roll(c, NY - st, 0))
                    w = pltpu.roll(beyond, (LANES + NZ - st - xs[i] * (2 * st)) % LANES, 1)
                    zl = jnp.where(lane % NZ < st, w, pltpu.roll(c, st, 1))
                    zh = jnp.where(lane % NZ >= NZ - st, w, pltpu.roll(c, LANES - st, 1))
                    hoods.append((c, loaded[i], loaded[i + 2], yl, yh, zl, zh))
            results = body(xs, hoods)
            if staged:
                for x, n in zip(xs, results):
                    packed = jnp.where(spot == x, pltpu.roll(n, x * (2 * st), 1), packed)
                for x, n in zip(xs, results):
                    ys[0, pl.ds(x, 1), :] = n[0:1, :]
                    ys[1, pl.ds(x, 1), :] = n[NY - 1:NY, :]
            return packed

        if staged:
            zs[...] = lax.fori_loop(0, planes // GROUP, step, jnp.zeros((NY, LANES), F32))
        else:
            lax.fori_loop(0, planes // GROUP, step, 0)

    def fine_nb(x, hood):
        c, xl, xh, yl, yh, zl, zh = hood
        return c, (
            (fx[x] * xl + fx[x + 1] * xh) + (fyl[x] * yl + fyh[x] * yh) + (fzl[x] * zl + fzh[x] * zh)
        )

    def coarse_nb(x, hood):
        c, xl, xh, yl, yh, zl, zh = hood
        return c, (
            (cfx[x] * xl + cfx[x + 1] * xh) + (cfyl[x] * yl + cfyh[x] * yh) + (cfzl[x] * zl + cfzh[x] * zh)
        )

    def is_colour(x, st, colour):
        return (row_ids() // st + lane_ids() // st + x + colour) % 2 == 0

    forward(0)
    forward(1)
    unpack(0, bv, 1)
    level_pass(PLANES, 1, lambda xs, hoods: [bv[x + 1] for x in xs])
    exchange(0, bv, PLANES)
    forward(2)

    def faces(xs, hoods):
        for x, (c, xl, xh, yl, yh, zl, zh) in zip(xs, hoods):
            fx[x] = 0.5 * (c + xl)
            fyl[x] = 0.5 * (c + yl)
            fyh[x] = 0.5 * (c + yh)
            fzl[x] = 0.5 * (c + zl)
            fzh[x] = 0.5 * (c + zh)

    level_pass(PLANES, 1, faces, staged=False, field=bv, e=0)
    fx[PLANES] = 0.5 * (bv[PLANES] + bv[PLANES + 1])

    unpack(1, ac, 0)

    @pl.loop(0, PLANES // 2)
    def _(i):
        x = 2 * i
        for o in range(2):
            d = ac[x + o] + (
                (fx[x + o] + fx[x + o + 1]) + (fyl[x + o] + fyh[x + o]) + (fzl[x + o] + fzh[x + o])
            )
            dg[x + o] = d
            rd[x + o] = 1.0 / d
        s = 0.0625
        wxl = s * pair_z(pair_y(fx[x]))
        wxh = s * pair_z(pair_y(fx[x + 2]))
        wyl = s * pair_z(even_y(fyl[x] + fyl[x + 1]))
        wyh = s * pair_z(odd_y(fyh[x] + fyh[x + 1]))
        wzl = s * pair_y(even_z(fzl[x] + fzl[x + 1]))
        wzh = s * pair_y(odd_z(fzh[x] + fzh[x + 1]))
        cfx[i] = wxl
        cfx[i + 1] = wxh
        cfyl[i] = wyl
        cfyh[i] = wyh
        cfzl[i] = wzl
        cfzh[i] = wzh
        ca = 0.125 * pair_z(pair_y(ac[x] + ac[x + 1]))
        crd[i] = 1.0 / (ca + ((wxl + wxh) + (wyl + wyh) + (wzl + wzh)))

    unpack(2, rh, 0)

    def store(field, xs, values):
        for x, n in zip(xs, values):
            field[x + 1] = n
        return values

    def first_red(xs, hoods):
        return store(v, xs, [jnp.where(is_colour(x, 1, 0), rh[x] * rd[x], 0.0) for x in xs])

    def half(e, colour):
        def update(xs, hoods):
            values = []
            for x, hood in zip(xs, hoods):
                c, nb = fine_nb(x, hood)
                values.append(jnp.where(is_colour(x, 1, colour), (rh[x] + nb) * rd[x], c))
            return store(v, xs, values)

        level_pass(PLANES, 1, update, field=v, e=e)

    level_pass(PLANES, 1, first_red)
    exchange(1, v, PLANES)
    half(1, 1)
    exchange(2, v, PLANES)

    def restrict(xs, hoods):
        for p in range(0, GROUP, 2):
            total = None
            for x, hood in zip(xs[p:p + 2], hoods[p:p + 2]):
                c, nb = fine_nb(x, hood)
                r = rh[x] - (dg[x] * c - nb)
                total = r if total is None else total + r
            cf[xs[p] // 2] = 0.125 * pair_z(pair_y(total))

    level_pass(PLANES, 1, restrict, staged=False, field=v, e=2)

    def first_coarse(xs, hoods):
        return store(cc, xs, [jnp.where(is_colour(x, 2, 0), cf[x] * crd[x], 0.0) for x in xs])

    level_pass(PLANES // 2, 2, first_coarse)

    @pl.loop(1, COARSE_HALVES)
    def _(h):
        e = 2 + h
        exchange(e, cc, PLANES // 2)

        def update(xs, hoods):
            values = []
            for x, hood in zip(xs, hoods):
                c, nb = coarse_nb(x, hood)
                values.append(jnp.where(is_colour(x, 2, h), (cf[x] + nb) * crd[x], c))
            return store(cc, xs, values)

        level_pass(PLANES // 2, 2, update, field=cc, e=e)

    def correct(xs, hoods):
        coarse = [cc[xs[p] // 2 + 1] for p in range(0, GROUP, 2)]
        return store(v, xs, [v[x + 1] + coarse[i // 2] for i, x in enumerate(xs)])

    level_pass(PLANES, 1, correct)
    exchange(10, v, PLANES)
    half(10, 0)
    exchange(11, v, PLANES)
    half(11, 1)
    exchange(12, v, PLANES)

    def finish(xs, hoods):
        for x, hood in zip(xs, hoods):
            c, nb = fine_nb(x, hood)
            r = rh[x] - (dg[x] * c - nb)
            for out, n in ((sol_out, c), (res_out, r)):
                out[x] = n[:, :NZ]
                out[x + PLANES] = pltpu.roll(n, NZ, 1)[:, :NZ]

    level_pass(PLANES, 1, finish, staged=False, field=v, e=12)

    @pl.loop(1, members)
    def _(k):
        peer = (me + k) % members
        place_copy(peer, k, me).wait_send()
        for f in range(3):
            copy1(f, peer, k, me).wait_send()
            copy2(f, peer, k, me).wait_send()


def solution(mesh):
    sizes = (mesh.shape["gx"], mesh.shape["gy"], mesh.shape["gz"])
    members = sizes[0] * sizes[1]
    rows = 256 // members

    def rows128(boxes):
        return boxes[0].reshape(4, 256, LANES).transpose(1, 0, 2).reshape(1024, LANES)

    def body(rhs_boxes, a_boxes, b_boxes, new_place):
        spot = jnp.where(jnp.arange(8)[:, None] < 4, jnp.tile(new_place[0], 2)[:, None], -1)
        spot = jnp.broadcast_to(spot, (8, LANES)).astype(jnp.int32)
        fine = pltpu.VMEM((PLANES, NY, LANES), F32)
        coarse = pltpu.VMEM((PLANES // 2, NY, LANES), F32)
        box = pltpu.VMEM((members, 4 * rows, LANES), F32)
        boxes = pltpu.VMEM((3, members, 4 * rows, LANES), F32)
        dma = pltpu.SemaphoreType.DMA
        return pl.pallas_call(
            functools.partial(kernel, sizes),
            out_shape=[jax.ShapeDtypeStruct((NX, NY, NZ), F32)] * 2,
            in_specs=[pl.BlockSpec(memory_space=pltpu.VMEM)] * 4,
            out_specs=[pl.BlockSpec(memory_space=pltpu.VMEM)] * 2,
            scratch_shapes=[
                pltpu.VMEM((members, 8, LANES), jnp.int32),
                pltpu.VMEM((8, LANES), jnp.int32),
                pltpu.SMEM((8, LANES), jnp.int32),
                box, box, box, boxes, boxes,
                pltpu.VMEM((PLANES + 2, NY, LANES), F32),
                fine, fine, fine, fine,
                pltpu.VMEM((PLANES + 1, NY, LANES), F32),
                fine, fine, fine, fine,
                pltpu.VMEM((PLANES + 2, NY, LANES), F32),
                pltpu.VMEM((PLANES // 2 + 2, NY, LANES), F32),
                coarse, coarse,
                pltpu.VMEM((PLANES // 2 + 1, NY, LANES), F32),
                coarse, coarse, coarse, coarse,
                pltpu.VMEM((EXCHANGES, 2, NY, LANES), F32),
                pltpu.VMEM((EXCHANGES, 2, PLANES, LANES), F32),
                pltpu.VMEM((EXCHANGES, 2, NY, LANES), F32),
                pltpu.VMEM((2, PLANES, LANES), F32),
                pltpu.VMEM((NY, LANES), F32),
                dma((members,)), dma((members,)),
                dma((3, members)), dma((3, members)),
                dma((3, members)), dma((3, members)),
                dma,
                dma((6,)), dma((EXCHANGES, 6)),
            ],
            compiler_params=pltpu.CompilerParams(
                collective_id=0, has_side_effects=True, vmem_limit_bytes=48 * 1024 * 1024
            ),
        )(spot, rows128(rhs_boxes), rows128(a_boxes), rows128(b_boxes))

    return jax.shard_map(
        body,
        mesh=mesh,
        in_specs=(
            P("gz", ("gx", "gy"), None),
            P("gz", ("gx", "gy"), None),
            P("gz", ("gx", "gy"), None),
            P("gz", ("gx", "gy")),
        ),
        out_specs=(P("gx", "gy", "gz"), P("gx", "gy", "gz")),
        check_vma=False,
    )
```

```python
import functools

import jax
import jax.numpy as jnp
from jax import lax
from jax.experimental import pallas as pl
from jax.experimental.pallas import tpu as pltpu
from jax.sharding import PartitionSpec as P

MESH = pl.DeviceIdType.MESH
NX, NY, NZ = 64, 32, 64
PLANES = NX // 2
LANES = 128
COARSE_HALVES = 8
EXCHANGES = 13
GROUP = 4
F32 = jnp.float32


def lane_ids():
    return lax.broadcasted_iota(jnp.int32, (NY, LANES), 1)


def row_ids():
    return lax.broadcasted_iota(jnp.int32, (NY, LANES), 0)


def pair_z(v):
    return v + jnp.where(lane_ids() % 2 == 0, pltpu.roll(v, LANES - 1, 1), pltpu.roll(v, 1, 1))


def pair_y(v):
    return v + jnp.where(row_ids() % 2 == 0, pltpu.roll(v, NY - 1, 0), pltpu.roll(v, 1, 0))


def even_y(v):
    return jnp.where(row_ids() % 2 == 0, v, pltpu.roll(v, 1, 0))


def odd_y(v):
    return jnp.where(row_ids() % 2 == 1, v, pltpu.roll(v, NY - 1, 0))


def even_z(v):
    return jnp.where(lane_ids() % 2 == 0, v, pltpu.roll(v, 1, 1))


def odd_z(v):
    return jnp.where(lane_ids() % 2 == 1, v, pltpu.roll(v, LANES - 1, 1))


def kernel(
    sizes,
    place_ref, rhs_in, a_in, b_in,
    sol_out, res_out,
    got_place, inv_vmem, inv_smem, got_b, got_a, got_rhs, sorted_, final,
    bv, rh, ac, dg, rd, fx, fyl, fyh, fzl, fzh, v,
    cc, cf, crd, cfx, cfyl, cfyh, cfzl, cfzh,
    hx, hy, hz, ys, zs,
    place_send, place_recv, send1, recv1, send2, recv2, inv_sem, halo_send, halo_recv,
):
    n_gx, n_gy, n_gz = sizes
    members = n_gx * n_gy
    rows = 256 // members
    slabs = rows // 8
    gx, gy, gz = lax.axis_index("gx"), lax.axis_index("gy"), lax.axis_index("gz")
    me = gx * n_gy + gy
    got = (got_b, got_a, got_rhs)

    def member(t):
        return (t // n_gy, t % n_gy, gz)

    @pl.loop(0, EXCHANGES)
    def _(e):
        for side in range(2):
            hx[e, side] = jnp.zeros((NY, LANES), F32)
            hy[e, side] = jnp.zeros((PLANES, LANES), F32)
            hz[e, side] = jnp.zeros((NY, LANES), F32)

    barrier = pltpu.get_barrier_semaphore()

    @pl.loop(1, members)
    def _(k):
        pl.semaphore_signal(barrier, inc=1, device_id=member((me + k) % members), device_id_type=MESH)

    @pl.when(gz > 0)
    def _():
        pl.semaphore_signal(barrier, inc=1, device_id=(gx, gy, gz - 1), device_id_type=MESH)

    @pl.when(gz < n_gz - 1)
    def _():
        pl.semaphore_signal(barrier, inc=1, device_id=(gx, gy, gz + 1), device_id_type=MESH)

    pl.semaphore_wait(
        barrier, members - 1 + (gz > 0).astype(jnp.int32) + (gz < n_gz - 1).astype(jnp.int32)
    )

    def place_copy(peer, k, slot):
        return pltpu.make_async_remote_copy(
            src_ref=place_ref, dst_ref=got_place.at[slot],
            send_sem=place_send.at[k], recv_sem=place_recv.at[slot],
            device_id=member(peer), device_id_type=MESH,
        )

    def copy1(f, peer, k, slot):
        return pltpu.make_async_remote_copy(
            src_ref=(b_in, a_in, rhs_in)[f].at[pl.ds(pl.multiple_of(peer * 4 * rows, 8), 4 * rows)],
            dst_ref=got[f].at[slot],
            send_sem=send1.at[f, k], recv_sem=recv1.at[f, slot],
            device_id=member(peer), device_id_type=MESH,
        )

    def copy2(f, peer, k, slot):
        return pltpu.make_async_remote_copy(
            src_ref=sorted_.at[f, peer], dst_ref=final.at[f, slot],
            send_sem=send2.at[f, k], recv_sem=recv2.at[f, slot],
            device_id=member(peer), device_id_type=MESH,
        )

    @pl.loop(1, members)
    def _(k):
        place_copy((me + k) % members, k, me).start()

    def own1(f):
        return pltpu.make_async_copy(
            (b_in, a_in, rhs_in)[f].at[pl.ds(pl.multiple_of(me * 4 * rows, 8), 4 * rows)],
            got[f].at[me], recv1.at[f, me],
        )

    def send_pieces(f):
        own1(f).start()

        @pl.loop(1, members)
        def _(k):
            copy1(f, (me + k) % members, k, me).start()

    send_pieces(0)
    send_pieces(1)
    got_place[me] = place_ref[...]

    @pl.loop(1, members)
    def _(k):
        place_copy((me + k) % members, k, (me + k) % members).wait_recv()

    lane8 = lax.broadcasted_iota(jnp.int32, (8, LANES), 1)
    row8 = lax.broadcasted_iota(jnp.int32, (8, LANES), 0)

    def find(src, total):
        here = (got_place[src] == lane8) & (row8 < 4)
        return jnp.maximum(total, jnp.where(here, src * 4 + row8, 0))

    owner = lax.fori_loop(0, members, find, jnp.zeros((8, LANES), jnp.int32))
    for shift in (4, 2, 1):
        owner = jnp.maximum(owner, pltpu.roll(owner, shift, 0))
    inv_vmem[...] = owner
    inv_copy = pltpu.make_async_copy(inv_vmem, inv_smem, inv_sem)
    inv_copy.start()
    inv_copy.wait()

    def forward(f):
        own1(f).wait()

        @pl.loop(1, members)
        def _(k):
            copy1(f, (me + k) % members, k, (me + k) % members).wait_recv()

        def pick(t, q):
            index = inv_smem[0, t * 4 + q]
            return got[f][index >> 2, pl.ds(index & 3, rows, stride=4), :]

        @pl.loop(1, members)
        def _(k):
            t = (me + k) % members
            for q in range(4):
                sorted_[f, t, q * rows:(q + 1) * rows, :] = pick(t, q)
            copy2(f, t, k, me).start()

        for q in range(4):
            final[f, me, q * rows:(q + 1) * rows, :] = pick(me, q)

    def unpack(f, out, first):
        @pl.loop(1, members)
        def _(k):
            copy2(f, (me + k) % members, k, (me + k) % members).wait_recv()

        @pl.loop(0, members)
        def _(j):
            for slab in range(slabs):
                tiles = [final[f, j, q * rows + slab * 8:q * rows + slab * 8 + 8, :] for q in range(4)]
                for yr in range(4):
                    whole = tiles[yr]
                    for q in range(4):
                        if q != yr:
                            turned = pltpu.roll(tiles[q], (32 * (q - yr)) % LANES, 1)
                            whole = jnp.where(lane8 // 32 == q, turned, whole)
                    out[j * slabs + slab + first, pl.ds(yr, 8, stride=4), :] = whole

    def exchange(e, field, planes, acts=("start", "wait")):
        for act in acts:
            for axis in range(3):
                for side in range(2):
                    d = axis * 2 + side
                    place, count = ((gx, n_gx), (gy, n_gy), (gz, n_gz))[axis]
                    there = place > 0 if side == 0 else place < count - 1
                    other = [gx, gy, gz]
                    other[axis] = place + (2 * side - 1)
                    if axis == 0:
                        src, dst = field.at[1 if side == 0 else planes], hx
                        to, mine = dst.at[e, 1 - side], dst.at[e, side]
                    elif axis == 1:
                        src = ys.at[side, pl.ds(0, planes)]
                        to, mine = hy.at[e, 1 - side, pl.ds(0, planes)], hy.at[e, side, pl.ds(0, planes)]
                    else:
                        src, to, mine = zs, hz.at[e, 1 - side], hz.at[e, side]

                    @pl.when(there)
                    def _():
                        out = pltpu.make_async_remote_copy(
                            src_ref=src, dst_ref=to, send_sem=halo_send.at[d],
                            recv_sem=halo_recv.at[e, axis * 2 + 1 - side],
                            device_id=tuple(other), device_id_type=MESH,
                        )
                        if act == "start":
                            out.start()
                        else:
                            out.wait_send()
                            pltpu.make_async_remote_copy(
                                src_ref=src, dst_ref=mine, send_sem=halo_send.at[d],
                                recv_sem=halo_recv.at[e, d],
                                device_id=tuple(other), device_id_type=MESH,
                            ).wait_recv()
        if "wait" not in acts:
            return
        low, lane = field[1], lane_ids()
        field[0] = pltpu.roll(jnp.where(lane >= NZ, hx[e, 0], field[planes]), NZ, 1)
        field[planes + 1] = pltpu.roll(jnp.where(lane < NZ, hx[e, 1], low), NZ, 1)

    def level_pass(planes, st, body, staged=True, field=None, e=None):
        lane, row = lane_ids(), row_ids()
        spot = ((lane + st) % NZ) // (2 * st)
        if e is not None:
            beyond = jnp.where((lane // st) % 2 == 0, hz[e, 1], pltpu.roll(hz[e, 0], 2 * st, 1))

        def step(g, packed):
            xs = [g * GROUP + i for i in range(GROUP)]
            hoods = [None] * GROUP
            if e is not None:
                loaded = [field[xs[0] + i] for i in range(GROUP + 2)]
                hoods = []
                for i in range(GROUP):
                    c = loaded[i + 1]
                    yl = jnp.where(row < st, hy[e, 0, pl.ds(xs[i], 1), :], pltpu.roll(c, st, 0))
                    yh = jnp.where(row >= NY - st, hy[e, 1, pl.ds(xs[i], 1), :], pltpu.roll(c, NY - st, 0))
                    w = pltpu.roll(beyond, (LANES + NZ - st - xs[i] * (2 * st)) % LANES, 1)
                    zl = jnp.where(lane % NZ < st, w, pltpu.roll(c, st, 1))
                    zh = jnp.where(lane % NZ >= NZ - st, w, pltpu.roll(c, LANES - st, 1))
                    hoods.append((c, loaded[i], loaded[i + 2], yl, yh, zl, zh))
            results = body(xs, hoods)
            if staged:
                for x, n in zip(xs, results):
                    packed = jnp.where(spot == x, pltpu.roll(n, x * (2 * st), 1), packed)
                for x, n in zip(xs, results):
                    ys[0, pl.ds(x, 1), :] = n[0:1, :]
                    ys[1, pl.ds(x, 1), :] = n[NY - 1:NY, :]
            return packed

        if staged:
            zs[...] = lax.fori_loop(0, planes // GROUP, step, jnp.zeros((NY, LANES), F32))
        else:
            lax.fori_loop(0, planes // GROUP, step, 0)

    def fine_nb(x, hood):
        c, xl, xh, yl, yh, zl, zh = hood
        return c, (
            (fx[x] * xl + fx[x + 1] * xh) + (fyl[x] * yl + fyh[x] * yh) + (fzl[x] * zl + fzh[x] * zh)
        )

    def coarse_nb(x, hood):
        c, xl, xh, yl, yh, zl, zh = hood
        return c, (
            (cfx[x] * xl + cfx[x + 1] * xh) + (cfyl[x] * yl + cfyh[x] * yh) + (cfzl[x] * zl + cfzh[x] * zh)
        )

    def is_colour(x, st, colour):
        return (row_ids() // st + lane_ids() // st + x + colour) % 2 == 0

    forward(0)
    send_pieces(2)
    forward(1)
    unpack(0, bv, 1)
    level_pass(PLANES, 1, lambda xs, hoods: [bv[x + 1] for x in xs])
    exchange(0, bv, PLANES, ("start",))
    forward(2)
    exchange(0, bv, PLANES, ("wait",))

    def faces(xs, hoods):
        for x, (c, xl, xh, yl, yh, zl, zh) in zip(xs, hoods):
            fx[x] = 0.5 * (c + xl)
            fyl[x] = 0.5 * (c + yl)
            fyh[x] = 0.5 * (c + yh)
            fzl[x] = 0.5 * (c + zl)
            fzh[x] = 0.5 * (c + zh)

    level_pass(PLANES, 1, faces, staged=False, field=bv, e=0)
    fx[PLANES] = 0.5 * (bv[PLANES] + bv[PLANES + 1])

    unpack(1, ac, 0)

    @pl.loop(0, PLANES // 2)
    def _(i):
        x = 2 * i
        for o in range(2):
            d = ac[x + o] + (
                (fx[x + o] + fx[x + o + 1]) + (fyl[x + o] + fyh[x + o]) + (fzl[x + o] + fzh[x + o])
            )
            dg[x + o] = d
            rd[x + o] = 1.0 / d
        s = 0.0625
        wxl = s * pair_z(pair_y(fx[x]))
        wxh = s * pair_z(pair_y(fx[x + 2]))
        wyl = s * pair_z(even_y(fyl[x] + fyl[x + 1]))
        wyh = s * pair_z(odd_y(fyh[x] + fyh[x + 1]))
        wzl = s * pair_y(even_z(fzl[x] + fzl[x + 1]))
        wzh = s * pair_y(odd_z(fzh[x] + fzh[x + 1]))
        cfx[i] = wxl
        cfx[i + 1] = wxh
        cfyl[i] = wyl
        cfyh[i] = wyh
        cfzl[i] = wzl
        cfzh[i] = wzh
        ca = 0.125 * pair_z(pair_y(ac[x] + ac[x + 1]))
        crd[i] = 1.0 / (ca + ((wxl + wxh) + (wyl + wyh) + (wzl + wzh)))

    unpack(2, rh, 0)

    def store(field, xs, values):
        for x, n in zip(xs, values):
            field[x + 1] = n
        return values

    def first_red(xs, hoods):
        return store(v, xs, [jnp.where(is_colour(x, 1, 0), rh[x] * rd[x], 0.0) for x in xs])

    def half(e, colour):
        def update(xs, hoods):
            values = []
            for x, hood in zip(xs, hoods):
                c, nb = fine_nb(x, hood)
                values.append(jnp.where(is_colour(x, 1, colour), (rh[x] + nb) * rd[x], c))
            return store(v, xs, values)

        level_pass(PLANES, 1, update, field=v, e=e)

    level_pass(PLANES, 1, first_red)
    exchange(1, v, PLANES)
    half(1, 1)
    exchange(2, v, PLANES)

    def restrict(xs, hoods):
        for p in range(0, GROUP, 2):
            total = None
            for x, hood in zip(xs[p:p + 2], hoods[p:p + 2]):
                c, nb = fine_nb(x, hood)
                r = rh[x] - (dg[x] * c - nb)
                total = r if total is None else total + r
            cf[xs[p] // 2] = 0.125 * pair_z(pair_y(total))

    level_pass(PLANES, 1, restrict, staged=False, field=v, e=2)

    def first_coarse(xs, hoods):
        return store(cc, xs, [jnp.where(is_colour(x, 2, 0), cf[x] * crd[x], 0.0) for x in xs])

    level_pass(PLANES // 2, 2, first_coarse)

    @pl.loop(1, COARSE_HALVES)
    def _(h):
        e = 2 + h
        exchange(e, cc, PLANES // 2)

        def update(xs, hoods):
            values = []
            for x, hood in zip(xs, hoods):
                c, nb = coarse_nb(x, hood)
                values.append(jnp.where(is_colour(x, 2, h), (cf[x] + nb) * crd[x], c))
            return store(cc, xs, values)

        level_pass(PLANES // 2, 2, update, field=cc, e=e)

    def correct(xs, hoods):
        coarse = [cc[xs[p] // 2 + 1] for p in range(0, GROUP, 2)]
        return store(v, xs, [v[x + 1] + coarse[i // 2] for i, x in enumerate(xs)])

    level_pass(PLANES, 1, correct)
    exchange(10, v, PLANES)
    half(10, 0)
    exchange(11, v, PLANES)
    half(11, 1)
    exchange(12, v, PLANES)

    def finish(xs, hoods):
        for x, hood in zip(xs, hoods):
            c, nb = fine_nb(x, hood)
            r = rh[x] - (dg[x] * c - nb)
            for out, n in ((sol_out, c), (res_out, r)):
                out[x] = n[:, :NZ]
                out[x + PLANES] = pltpu.roll(n, NZ, 1)[:, :NZ]

    level_pass(PLANES, 1, finish, staged=False, field=v, e=12)

    @pl.loop(1, members)
    def _(k):
        peer = (me + k) % members
        place_copy(peer, k, me).wait_send()
        for f in range(3):
            copy1(f, peer, k, me).wait_send()
            copy2(f, peer, k, me).wait_send()


def solution(mesh):
    sizes = (mesh.shape["gx"], mesh.shape["gy"], mesh.shape["gz"])
    members = sizes[0] * sizes[1]
    rows = 256 // members

    def rows128(boxes):
        return boxes[0].reshape(4, 256, LANES).transpose(1, 0, 2).reshape(1024, LANES)

    def body(rhs_boxes, a_boxes, b_boxes, new_place):
        spot = jnp.where(jnp.arange(8)[:, None] < 4, jnp.tile(new_place[0], 2)[:, None], -1)
        spot = jnp.broadcast_to(spot, (8, LANES)).astype(jnp.int32)
        fine = pltpu.VMEM((PLANES, NY, LANES), F32)
        coarse = pltpu.VMEM((PLANES // 2, NY, LANES), F32)
        box = pltpu.VMEM((members, 4 * rows, LANES), F32)
        boxes = pltpu.VMEM((3, members, 4 * rows, LANES), F32)
        dma = pltpu.SemaphoreType.DMA
        return pl.pallas_call(
            functools.partial(kernel, sizes),
            out_shape=[jax.ShapeDtypeStruct((NX, NY, NZ), F32)] * 2,
            in_specs=[pl.BlockSpec(memory_space=pltpu.VMEM)] + [pl.BlockSpec(memory_space=pltpu.HBM)] * 3,
            out_specs=[pl.BlockSpec(memory_space=pltpu.VMEM)] * 2,
            scratch_shapes=[
                pltpu.VMEM((members, 8, LANES), jnp.int32),
                pltpu.VMEM((8, LANES), jnp.int32),
                pltpu.SMEM((8, LANES), jnp.int32),
                box, box, box, boxes, boxes,
                pltpu.VMEM((PLANES + 2, NY, LANES), F32),
                fine, fine, fine, fine,
                pltpu.VMEM((PLANES + 1, NY, LANES), F32),
                fine, fine, fine, fine,
                pltpu.VMEM((PLANES + 2, NY, LANES), F32),
                pltpu.VMEM((PLANES // 2 + 2, NY, LANES), F32),
                coarse, coarse,
                pltpu.VMEM((PLANES // 2 + 1, NY, LANES), F32),
                coarse, coarse, coarse, coarse,
                pltpu.VMEM((EXCHANGES, 2, NY, LANES), F32),
                pltpu.VMEM((EXCHANGES, 2, PLANES, LANES), F32),
                pltpu.VMEM((EXCHANGES, 2, NY, LANES), F32),
                pltpu.VMEM((2, PLANES, LANES), F32),
                pltpu.VMEM((NY, LANES), F32),
                dma((members,)), dma((members,)),
                dma((3, members)), dma((3, members)),
                dma((3, members)), dma((3, members)),
                dma,
                dma((6,)), dma((EXCHANGES, 6)),
            ],
            compiler_params=pltpu.CompilerParams(
                collective_id=0, has_side_effects=True, vmem_limit_bytes=48 * 1024 * 1024
            ),
        )(spot, rows128(rhs_boxes), rows128(a_boxes), rows128(b_boxes))

    return jax.shard_map(
        body,
        mesh=mesh,
        in_specs=(
            P("gz", ("gx", "gy"), None),
            P("gz", ("gx", "gy"), None),
            P("gz", ("gx", "gy"), None),
            P("gz", ("gx", "gy")),
        ),
        out_specs=(P("gx", "gy", "gz"), P("gx", "gy", "gz")),
        check_vma=False,
    )
```

```python
import functools

import jax
import jax.numpy as jnp
from jax import lax
from jax.experimental import pallas as pl
from jax.experimental.pallas import tpu as pltpu
from jax.sharding import PartitionSpec as P

MESH = pl.DeviceIdType.MESH
NX, NY, NZ = 64, 32, 64
PLANES = NX // 2
LANES = 128
COARSE_HALVES = 8
EXCHANGES = 13
GROUP = 8
F32 = jnp.float32


def lane_ids():
    return lax.broadcasted_iota(jnp.int32, (NY, LANES), 1)


def row_ids():
    return lax.broadcasted_iota(jnp.int32, (NY, LANES), 0)


def pair_z(v):
    return v + jnp.where(lane_ids() % 2 == 0, pltpu.roll(v, LANES - 1, 1), pltpu.roll(v, 1, 1))


def pair_y(v):
    return v + jnp.where(row_ids() % 2 == 0, pltpu.roll(v, NY - 1, 0), pltpu.roll(v, 1, 0))


def even_y(v):
    return jnp.where(row_ids() % 2 == 0, v, pltpu.roll(v, 1, 0))


def odd_y(v):
    return jnp.where(row_ids() % 2 == 1, v, pltpu.roll(v, NY - 1, 0))


def even_z(v):
    return jnp.where(lane_ids() % 2 == 0, v, pltpu.roll(v, 1, 1))


def odd_z(v):
    return jnp.where(lane_ids() % 2 == 1, v, pltpu.roll(v, LANES - 1, 1))


def kernel(
    sizes,
    place_ref, rhs_in, a_in, b_in,
    sol_out, res_out,
    got_place, inv_vmem, inv_smem, got_b, got_a, got_rhs, sorted_, final,
    bv, rh, ac, dg, rd, fx, fyl, fyh, fzl, fzh, v,
    cc, cf, crd, cfx, cfyl, cfyh, cfzl, cfzh,
    hx, hy, hz, ys, zs,
    place_send, place_recv, send1, recv1, send2, recv2, inv_sem, halo_send, halo_recv,
):
    n_gx, n_gy, n_gz = sizes
    members = n_gx * n_gy
    rows = 256 // members
    slabs = rows // 8
    gx, gy, gz = lax.axis_index("gx"), lax.axis_index("gy"), lax.axis_index("gz")
    me = gx * n_gy + gy
    got = (got_b, got_a, got_rhs)

    def member(t):
        return (t // n_gy, t % n_gy, gz)

    @pl.loop(0, EXCHANGES)
    def _(e):
        for side in range(2):
            hx[e, side] = jnp.zeros((NY, LANES), F32)
            hy[e, side] = jnp.zeros((PLANES, LANES), F32)
            hz[e, side] = jnp.zeros((NY, LANES), F32)

    barrier = pltpu.get_barrier_semaphore()

    @pl.loop(1, members)
    def _(k):
        pl.semaphore_signal(barrier, inc=1, device_id=member((me + k) % members), device_id_type=MESH)

    @pl.when(gz > 0)
    def _():
        pl.semaphore_signal(barrier, inc=1, device_id=(gx, gy, gz - 1), device_id_type=MESH)

    @pl.when(gz < n_gz - 1)
    def _():
        pl.semaphore_signal(barrier, inc=1, device_id=(gx, gy, gz + 1), device_id_type=MESH)

    pl.semaphore_wait(
        barrier, members - 1 + (gz > 0).astype(jnp.int32) + (gz < n_gz - 1).astype(jnp.int32)
    )

    def place_copy(peer, k, slot):
        return pltpu.make_async_remote_copy(
            src_ref=place_ref, dst_ref=got_place.at[slot],
            send_sem=place_send.at[k], recv_sem=place_recv.at[slot],
            device_id=member(peer), device_id_type=MESH,
        )

    def copy1(f, peer, k, slot):
        return pltpu.make_async_remote_copy(
            src_ref=(b_in, a_in, rhs_in)[f].at[pl.ds(pl.multiple_of(peer * 4 * rows, 8), 4 * rows)],
            dst_ref=got[f].at[slot],
            send_sem=send1.at[f, k], recv_sem=recv1.at[f, slot],
            device_id=member(peer), device_id_type=MESH,
        )

    def copy2(f, peer, k, slot):
        return pltpu.make_async_remote_copy(
            src_ref=sorted_.at[f, peer], dst_ref=final.at[f, slot],
            send_sem=send2.at[f, k], recv_sem=recv2.at[f, slot],
            device_id=member(peer), device_id_type=MESH,
        )

    @pl.loop(1, members)
    def _(k):
        place_copy((me + k) % members, k, me).start()

    def own1(f):
        return pltpu.make_async_copy(
            (b_in, a_in, rhs_in)[f].at[pl.ds(pl.multiple_of(me * 4 * rows, 8), 4 * rows)],
            got[f].at[me], recv1.at[f, me],
        )

    def send_pieces(f):
        own1(f).start()

        @pl.loop(1, members)
        def _(k):
            copy1(f, (me + k) % members, k, me).start()

    send_pieces(0)
    send_pieces(1)
    got_place[me] = place_ref[...]

    @pl.loop(1, members)
    def _(k):
        place_copy((me + k) % members, k, (me + k) % members).wait_recv()

    lane8 = lax.broadcasted_iota(jnp.int32, (8, LANES), 1)
    row8 = lax.broadcasted_iota(jnp.int32, (8, LANES), 0)

    def find(src, total):
        here = (got_place[src] == lane8) & (row8 < 4)
        return jnp.maximum(total, jnp.where(here, src * 4 + row8, 0))

    owner = lax.fori_loop(0, members, find, jnp.zeros((8, LANES), jnp.int32))
    for shift in (4, 2, 1):
        owner = jnp.maximum(owner, pltpu.roll(owner, shift, 0))
    inv_vmem[...] = owner
    inv_copy = pltpu.make_async_copy(inv_vmem, inv_smem, inv_sem)
    inv_copy.start()
    inv_copy.wait()

    def forward(f):
        own1(f).wait()

        @pl.loop(1, members)
        def _(k):
            copy1(f, (me + k) % members, k, (me + k) % members).wait_recv()

        def pick(t, q):
            index = inv_smem[0, t * 4 + q]
            return got[f][index >> 2, pl.ds(index & 3, rows, stride=4), :]

        @pl.loop(1, members)
        def _(k):
            t = (me + k) % members
            for q in range(4):
                sorted_[f, t, q * rows:(q + 1) * rows, :] = pick(t, q)
            copy2(f, t, k, me).start()

        for q in range(4):
            final[f, me, q * rows:(q + 1) * rows, :] = pick(me, q)

    def unpack(f, out, first):
        @pl.loop(1, members)
        def _(k):
            copy2(f, (me + k) % members, k, (me + k) % members).wait_recv()

        @pl.loop(0, members)
        def _(j):
            for slab in range(slabs):
                tiles = [final[f, j, q * rows + slab * 8:q * rows + slab * 8 + 8, :] for q in range(4)]
                for yr in range(4):
                    whole = tiles[yr]
                    for q in range(4):
                        if q != yr:
                            turned = pltpu.roll(tiles[q], (32 * (q - yr)) % LANES, 1)
                            whole = jnp.where(lane8 // 32 == q, turned, whole)
                    out[j * slabs + slab + first, pl.ds(yr, 8, stride=4), :] = whole

    def exchange(e, field, planes, acts=("start", "wait")):
        for act in acts:
            for axis in (1, 0, 2):
                for side in range(2):
                    d = axis * 2 + side
                    place, count = ((gx, n_gx), (gy, n_gy), (gz, n_gz))[axis]
                    there = place > 0 if side == 0 else place < count - 1
                    other = [gx, gy, gz]
                    other[axis] = place + (2 * side - 1)
                    if axis == 0:
                        src, dst = field.at[1 if side == 0 else planes], hx
                        to, mine = dst.at[e, 1 - side], dst.at[e, side]
                    elif axis == 1:
                        src = ys.at[side, pl.ds(0, planes)]
                        to, mine = hy.at[e, 1 - side, pl.ds(0, planes)], hy.at[e, side, pl.ds(0, planes)]
                    else:
                        src, to, mine = zs, hz.at[e, 1 - side], hz.at[e, side]

                    @pl.when(there)
                    def _():
                        out = pltpu.make_async_remote_copy(
                            src_ref=src, dst_ref=to, send_sem=halo_send.at[d],
                            recv_sem=halo_recv.at[e, axis * 2 + 1 - side],
                            device_id=tuple(other), device_id_type=MESH,
                        )
                        if act == "start":
                            out.start()
                        else:
                            out.wait_send()
                            pltpu.make_async_remote_copy(
                                src_ref=src, dst_ref=mine, send_sem=halo_send.at[d],
                                recv_sem=halo_recv.at[e, d],
                                device_id=tuple(other), device_id_type=MESH,
                            ).wait_recv()
        if "wait" not in acts:
            return
        low, lane = field[1], lane_ids()
        field[0] = pltpu.roll(jnp.where(lane >= NZ, hx[e, 0], field[planes]), NZ, 1)
        field[planes + 1] = pltpu.roll(jnp.where(lane < NZ, hx[e, 1], low), NZ, 1)

    def level_pass(planes, st, body, staged=True, field=None, e=None):
        lane, row = lane_ids(), row_ids()
        spot = ((lane + st) % NZ) // (2 * st)
        if e is not None:
            beyond = jnp.where((lane // st) % 2 == 0, hz[e, 1], pltpu.roll(hz[e, 0], 2 * st, 1))

        def step(g, packed):
            xs = [g * GROUP + i for i in range(GROUP)]
            hoods = [None] * GROUP
            if e is not None:
                loaded = [field[xs[0] + i] for i in range(GROUP + 2)]
                hoods = []
                for i in range(GROUP):
                    c = loaded[i + 1]
                    yl = jnp.where(row < st, hy[e, 0, pl.ds(xs[i], 1), :], pltpu.roll(c, st, 0))
                    yh = jnp.where(row >= NY - st, hy[e, 1, pl.ds(xs[i], 1), :], pltpu.roll(c, NY - st, 0))
                    w = pltpu.roll(beyond, (LANES + NZ - st - xs[i] * (2 * st)) % LANES, 1)
                    zl = jnp.where(lane % NZ < st, w, pltpu.roll(c, st, 1))
                    zh = jnp.where(lane % NZ >= NZ - st, w, pltpu.roll(c, LANES - st, 1))
                    hoods.append((c, loaded[i], loaded[i + 2], yl, yh, zl, zh))
            results = body(xs, hoods)
            if staged:
                for x, n in zip(xs, results):
                    packed = jnp.where(spot == x, pltpu.roll(n, x * (2 * st), 1), packed)
                for x, n in zip(xs, results):
                    ys[0, pl.ds(x, 1), :] = n[0:1, :]
                    ys[1, pl.ds(x, 1), :] = n[NY - 1:NY, :]
            return packed

        if staged:
            zs[...] = lax.fori_loop(0, planes // GROUP, step, jnp.zeros((NY, LANES), F32))
        else:
            lax.fori_loop(0, planes // GROUP, step, 0)

    def fine_nb(x, hood):
        c, xl, xh, yl, yh, zl, zh = hood
        return c, (
            (fx[x] * xl + fx[x + 1] * xh) + (fyl[x] * yl + fyh[x] * yh) + (fzl[x] * zl + fzh[x] * zh)
        )

    def coarse_nb(x, hood):
        c, xl, xh, yl, yh, zl, zh = hood
        return c, (
            (cfx[x] * xl + cfx[x + 1] * xh) + (cfyl[x] * yl + cfyh[x] * yh) + (cfzl[x] * zl + cfzh[x] * zh)
        )

    def is_colour(x, st, colour):
        return (row_ids() // st + lane_ids() // st + x + colour) % 2 == 0

    forward(0)
    send_pieces(2)
    forward(1)
    unpack(0, bv, 1)
    level_pass(PLANES, 1, lambda xs, hoods: [bv[x + 1] for x in xs])
    exchange(0, bv, PLANES, ("start",))
    forward(2)
    exchange(0, bv, PLANES, ("wait",))

    def faces(xs, hoods):
        for x, (c, xl, xh, yl, yh, zl, zh) in zip(xs, hoods):
            fx[x] = 0.5 * (c + xl)
            fyl[x] = 0.5 * (c + yl)
            fyh[x] = 0.5 * (c + yh)
            fzl[x] = 0.5 * (c + zl)
            fzh[x] = 0.5 * (c + zh)

    level_pass(PLANES, 1, faces, staged=False, field=bv, e=0)
    fx[PLANES] = 0.5 * (bv[PLANES] + bv[PLANES + 1])

    unpack(1, ac, 0)

    @pl.loop(0, PLANES // 2)
    def _(i):
        x = 2 * i
        for o in range(2):
            d = ac[x + o] + (
                (fx[x + o] + fx[x + o + 1]) + (fyl[x + o] + fyh[x + o]) + (fzl[x + o] + fzh[x + o])
            )
            dg[x + o] = d
            rd[x + o] = 1.0 / d
        s = 0.0625
        wxl = s * pair_z(pair_y(fx[x]))
        wxh = s * pair_z(pair_y(fx[x + 2]))
        wyl = s * pair_z(even_y(fyl[x] + fyl[x + 1]))
        wyh = s * pair_z(odd_y(fyh[x] + fyh[x + 1]))
        wzl = s * pair_y(even_z(fzl[x] + fzl[x + 1]))
        wzh = s * pair_y(odd_z(fzh[x] + fzh[x + 1]))
        cfx[i] = wxl
        cfx[i + 1] = wxh
        cfyl[i] = wyl
        cfyh[i] = wyh
        cfzl[i] = wzl
        cfzh[i] = wzh
        ca = 0.125 * pair_z(pair_y(ac[x] + ac[x + 1]))
        crd[i] = 1.0 / (ca + ((wxl + wxh) + (wyl + wyh) + (wzl + wzh)))

    unpack(2, rh, 0)

    def store(field, xs, values):
        for x, n in zip(xs, values):
            field[x + 1] = n
        return values

    def first_red(xs, hoods):
        return store(v, xs, [jnp.where(is_colour(x, 1, 0), rh[x] * rd[x], 0.0) for x in xs])

    def half(e, colour):
        def update(xs, hoods):
            values = []
            for x, hood in zip(xs, hoods):
                c, nb = fine_nb(x, hood)
                values.append(jnp.where(is_colour(x, 1, colour), (rh[x] + nb) * rd[x], c))
            return store(v, xs, values)

        level_pass(PLANES, 1, update, field=v, e=e)

    level_pass(PLANES, 1, first_red)
    exchange(1, v, PLANES)
    half(1, 1)
    exchange(2, v, PLANES)

    def restrict(xs, hoods):
        for p in range(0, GROUP, 2):
            total = None
            for x, hood in zip(xs[p:p + 2], hoods[p:p + 2]):
                c, nb = fine_nb(x, hood)
                r = rh[x] - (dg[x] * c - nb)
                total = r if total is None else total + r
            cf[xs[p] // 2] = 0.125 * pair_z(pair_y(total))

    level_pass(PLANES, 1, restrict, staged=False, field=v, e=2)

    def first_coarse(xs, hoods):
        return store(cc, xs, [jnp.where(is_colour(x, 2, 0), cf[x] * crd[x], 0.0) for x in xs])

    level_pass(PLANES // 2, 2, first_coarse)

    @pl.loop(1, COARSE_HALVES)
    def _(h):
        e = 2 + h
        exchange(e, cc, PLANES // 2)

        def update(xs, hoods):
            values = []
            for x, hood in zip(xs, hoods):
                c, nb = coarse_nb(x, hood)
                values.append(jnp.where(is_colour(x, 2, h), (cf[x] + nb) * crd[x], c))
            return store(cc, xs, values)

        level_pass(PLANES // 2, 2, update, field=cc, e=e)

    def correct(xs, hoods):
        coarse = [cc[xs[p] // 2 + 1] for p in range(0, GROUP, 2)]
        return store(v, xs, [v[x + 1] + coarse[i // 2] for i, x in enumerate(xs)])

    level_pass(PLANES, 1, correct)
    exchange(10, v, PLANES)
    half(10, 0)
    exchange(11, v, PLANES)
    half(11, 1)
    exchange(12, v, PLANES)

    def finish(xs, hoods):
        for x, hood in zip(xs, hoods):
            c, nb = fine_nb(x, hood)
            r = rh[x] - (dg[x] * c - nb)
            for out, n in ((sol_out, c), (res_out, r)):
                out[x] = n[:, :NZ]
                out[x + PLANES] = pltpu.roll(n, NZ, 1)[:, :NZ]

    level_pass(PLANES, 1, finish, staged=False, field=v, e=12)

    @pl.loop(1, members)
    def _(k):
        peer = (me + k) % members
        place_copy(peer, k, me).wait_send()
        for f in range(3):
            copy1(f, peer, k, me).wait_send()
            copy2(f, peer, k, me).wait_send()


def solution(mesh):
    sizes = (mesh.shape["gx"], mesh.shape["gy"], mesh.shape["gz"])
    members = sizes[0] * sizes[1]
    rows = 256 // members

    def rows128(boxes):
        return boxes[0].reshape(4, 256, LANES).transpose(1, 0, 2).reshape(1024, LANES)

    def body(rhs_boxes, a_boxes, b_boxes, new_place):
        spot = jnp.where(jnp.arange(8)[:, None] < 4, jnp.tile(new_place[0], 2)[:, None], -1)
        spot = jnp.broadcast_to(spot, (8, LANES)).astype(jnp.int32)
        fine = pltpu.VMEM((PLANES, NY, LANES), F32)
        coarse = pltpu.VMEM((PLANES // 2, NY, LANES), F32)
        box = pltpu.VMEM((members, 4 * rows, LANES), F32)
        boxes = pltpu.VMEM((3, members, 4 * rows, LANES), F32)
        dma = pltpu.SemaphoreType.DMA
        return pl.pallas_call(
            functools.partial(kernel, sizes),
            out_shape=[jax.ShapeDtypeStruct((NX, NY, NZ), F32)] * 2,
            in_specs=[pl.BlockSpec(memory_space=pltpu.VMEM)] + [pl.BlockSpec(memory_space=pltpu.HBM)] * 3,
            out_specs=[pl.BlockSpec(memory_space=pltpu.VMEM)] * 2,
            scratch_shapes=[
                pltpu.VMEM((members, 8, LANES), jnp.int32),
                pltpu.VMEM((8, LANES), jnp.int32),
                pltpu.SMEM((8, LANES), jnp.int32),
                box, box, box, boxes, boxes,
                pltpu.VMEM((PLANES + 2, NY, LANES), F32),
                fine, fine, fine, fine,
                pltpu.VMEM((PLANES + 1, NY, LANES), F32),
                fine, fine, fine, fine,
                pltpu.VMEM((PLANES + 2, NY, LANES), F32),
                pltpu.VMEM((PLANES // 2 + 2, NY, LANES), F32),
                coarse, coarse,
                pltpu.VMEM((PLANES // 2 + 1, NY, LANES), F32),
                coarse, coarse, coarse, coarse,
                pltpu.VMEM((EXCHANGES, 2, NY, LANES), F32),
                pltpu.VMEM((EXCHANGES, 2, PLANES, LANES), F32),
                pltpu.VMEM((EXCHANGES, 2, NY, LANES), F32),
                pltpu.VMEM((2, PLANES, LANES), F32),
                pltpu.VMEM((NY, LANES), F32),
                dma((members,)), dma((members,)),
                dma((3, members)), dma((3, members)),
                dma((3, members)), dma((3, members)),
                dma,
                dma((6,)), dma((EXCHANGES, 6)),
            ],
            compiler_params=pltpu.CompilerParams(
                collective_id=0, has_side_effects=True, vmem_limit_bytes=60 * 1024 * 1024
            ),
        )(spot, rows128(rhs_boxes), rows128(a_boxes), rows128(b_boxes))

    return jax.shard_map(
        body,
        mesh=mesh,
        in_specs=(
            P("gz", ("gx", "gy"), None),
            P("gz", ("gx", "gy"), None),
            P("gz", ("gx", "gy"), None),
            P("gz", ("gx", "gy")),
        ),
        out_specs=(P("gx", "gy", "gz"), P("gx", "gy", "gz")),
        check_vma=False,
    )
```

```python
import functools

import jax
import jax.numpy as jnp
from jax import lax
from jax.experimental import pallas as pl
from jax.experimental.pallas import tpu as pltpu
from jax.sharding import PartitionSpec as P

MESH = pl.DeviceIdType.MESH
NX, NY, NZ = 64, 32, 64
PLANES = NX // 2
LANES = 128
COARSE_HALVES = 8
EXCHANGES = 13
GROUP = 8
F32 = jnp.float32


def lane_ids():
    return lax.broadcasted_iota(jnp.int32, (NY, LANES), 1)


def row_ids():
    return lax.broadcasted_iota(jnp.int32, (NY, LANES), 0)


def pair_z(v):
    return v + jnp.where(lane_ids() % 2 == 0, pltpu.roll(v, LANES - 1, 1), pltpu.roll(v, 1, 1))


def pair_y(v):
    return v + jnp.where(row_ids() % 2 == 0, pltpu.roll(v, NY - 1, 0), pltpu.roll(v, 1, 0))


def even_y(v):
    return jnp.where(row_ids() % 2 == 0, v, pltpu.roll(v, 1, 0))


def odd_y(v):
    return jnp.where(row_ids() % 2 == 1, v, pltpu.roll(v, NY - 1, 0))


def even_z(v):
    return jnp.where(lane_ids() % 2 == 0, v, pltpu.roll(v, 1, 1))


def odd_z(v):
    return jnp.where(lane_ids() % 2 == 1, v, pltpu.roll(v, LANES - 1, 1))


def kernel(
    sizes,
    place_ref, rhs_in, a_in, b_in,
    sol_out, res_out,
    got_place, inv_vmem, inv_smem, got_b, got_a, got_rhs, sorted_, final,
    bv, rh, ac, dg, rd, fx, fyl, fyh, fzl, fzh, v,
    cc, cf, crd, cfx, cfyl, cfyh, cfzl, cfzh,
    hx, hy, hz, ys, zs,
    place_send, place_recv, send1, recv1, send2, recv2, inv_sem, halo_send, halo_recv,
):
    n_gx, n_gy, n_gz = sizes
    members = n_gx * n_gy
    rows = 256 // members
    slabs = rows // 8
    gx, gy, gz = lax.axis_index("gx"), lax.axis_index("gy"), lax.axis_index("gz")
    me = gx * n_gy + gy
    got = (got_b, got_a, got_rhs)

    def partner(k):
        return (me + 1 + (k + members // 2 - 2) % (members - 1)) % members

    def sender(k):
        return (me + members - 1 - (k + members // 2 - 2) % (members - 1)) % members

    def member(t):
        return (t // n_gy, t % n_gy, gz)

    @pl.loop(0, EXCHANGES)
    def _(e):
        for side in range(2):
            hx[e, side] = jnp.zeros((NY, LANES), F32)
            hy[e, side] = jnp.zeros((PLANES, LANES), F32)
            hz[e, side] = jnp.zeros((NY, LANES), F32)

    barrier = pltpu.get_barrier_semaphore()

    @pl.loop(1, members)
    def _(k):
        pl.semaphore_signal(barrier, inc=1, device_id=member((me + k) % members), device_id_type=MESH)

    @pl.when(gz > 0)
    def _():
        pl.semaphore_signal(barrier, inc=1, device_id=(gx, gy, gz - 1), device_id_type=MESH)

    @pl.when(gz < n_gz - 1)
    def _():
        pl.semaphore_signal(barrier, inc=1, device_id=(gx, gy, gz + 1), device_id_type=MESH)

    pl.semaphore_wait(
        barrier, members - 1 + (gz > 0).astype(jnp.int32) + (gz < n_gz - 1).astype(jnp.int32)
    )

    def place_copy(peer, k, slot):
        return pltpu.make_async_remote_copy(
            src_ref=place_ref, dst_ref=got_place.at[slot],
            send_sem=place_send.at[k], recv_sem=place_recv.at[slot],
            device_id=member(peer), device_id_type=MESH,
        )

    def copy1(f, peer, k, slot):
        return pltpu.make_async_remote_copy(
            src_ref=(b_in, a_in, rhs_in)[f].at[pl.ds(pl.multiple_of(peer * 4 * rows, 8), 4 * rows)],
            dst_ref=got[f].at[slot],
            send_sem=send1.at[f, k], recv_sem=recv1.at[f, slot],
            device_id=member(peer), device_id_type=MESH,
        )

    def copy2(f, peer, k, slot):
        return pltpu.make_async_remote_copy(
            src_ref=sorted_.at[f, peer], dst_ref=final.at[f, slot],
            send_sem=send2.at[f, k], recv_sem=recv2.at[f, slot],
            device_id=member(peer), device_id_type=MESH,
        )

    @pl.loop(1, members)
    def _(k):
        place_copy(partner(k), k, me).start()

    def own1(f):
        return pltpu.make_async_copy(
            (b_in, a_in, rhs_in)[f].at[pl.ds(pl.multiple_of(me * 4 * rows, 8), 4 * rows)],
            got[f].at[me], recv1.at[f, me],
        )

    def send_pieces(f):
        own1(f).start()

        @pl.loop(1, members)
        def _(k):
            copy1(f, partner(k), k, me).start()

    send_pieces(0)
    send_pieces(1)
    got_place[me] = place_ref[...]

    @pl.loop(1, members)
    def _(k):
        place_copy((me + k) % members, k, (me + k) % members).wait_recv()

    lane8 = lax.broadcasted_iota(jnp.int32, (8, LANES), 1)
    row8 = lax.broadcasted_iota(jnp.int32, (8, LANES), 0)

    def find(src, total):
        here = (got_place[src] == lane8) & (row8 < 4)
        return jnp.maximum(total, jnp.where(here, src * 4 + row8, 0))

    owner = lax.fori_loop(0, members, find, jnp.zeros((8, LANES), jnp.int32))
    for shift in (4, 2, 1):
        owner = jnp.maximum(owner, pltpu.roll(owner, shift, 0))
    inv_vmem[...] = owner
    inv_copy = pltpu.make_async_copy(inv_vmem, inv_smem, inv_sem)
    inv_copy.start()
    inv_copy.wait()

    def forward(f):
        own1(f).wait()

        @pl.loop(1, members)
        def _(k):
            copy1(f, (me + k) % members, k, (me + k) % members).wait_recv()

        def pick(t, q):
            index = inv_smem[0, t * 4 + q]
            return got[f][index >> 2, pl.ds(index & 3, rows, stride=4), :]

        @pl.loop(1, members)
        def _(k):
            t = partner(k)
            for q in range(4):
                sorted_[f, t, q * rows:(q + 1) * rows, :] = pick(t, q)
            copy2(f, t, k, me).start()

        for q in range(4):
            final[f, me, q * rows:(q + 1) * rows, :] = pick(me, q)

    def unpack(f, out, first):
        def one(j):
            for slab in range(slabs):
                tiles = [final[f, j, q * rows + slab * 8:q * rows + slab * 8 + 8, :] for q in range(4)]
                for yr in range(4):
                    whole = tiles[yr]
                    for q in range(4):
                        if q != yr:
                            turned = pltpu.roll(tiles[q], (32 * (q - yr)) % LANES, 1)
                            whole = jnp.where(lane8 // 32 == q, turned, whole)
                    out[j * slabs + slab + first, pl.ds(yr, 8, stride=4), :] = whole

        one(me)

        @pl.loop(1, members)
        def _(k):
            j = sender(k)
            copy2(f, j, k, j).wait_recv()
            one(j)

    def exchange(e, field, planes, acts=("start", "wait")):
        for act in acts:
            for axis in (1, 0, 2):
                for side in range(2):
                    d = axis * 2 + side
                    place, count = ((gx, n_gx), (gy, n_gy), (gz, n_gz))[axis]
                    there = place > 0 if side == 0 else place < count - 1
                    other = [gx, gy, gz]
                    other[axis] = place + (2 * side - 1)
                    if axis == 0:
                        src, dst = field.at[1 if side == 0 else planes], hx
                        to, mine = dst.at[e, 1 - side], dst.at[e, side]
                    elif axis == 1:
                        src = ys.at[side, pl.ds(0, planes)]
                        to, mine = hy.at[e, 1 - side, pl.ds(0, planes)], hy.at[e, side, pl.ds(0, planes)]
                    else:
                        src, to, mine = zs, hz.at[e, 1 - side], hz.at[e, side]

                    @pl.when(there)
                    def _():
                        out = pltpu.make_async_remote_copy(
                            src_ref=src, dst_ref=to, send_sem=halo_send.at[d],
                            recv_sem=halo_recv.at[e, axis * 2 + 1 - side],
                            device_id=tuple(other), device_id_type=MESH,
                        )
                        if act == "start":
                            out.start()
                        else:
                            out.wait_send()
                            pltpu.make_async_remote_copy(
                                src_ref=src, dst_ref=mine, send_sem=halo_send.at[d],
                                recv_sem=halo_recv.at[e, d],
                                device_id=tuple(other), device_id_type=MESH,
                            ).wait_recv()
        if "wait" not in acts:
            return
        low, lane = field[1], lane_ids()
        field[0] = pltpu.roll(jnp.where(lane >= NZ, hx[e, 0], field[planes]), NZ, 1)
        field[planes + 1] = pltpu.roll(jnp.where(lane < NZ, hx[e, 1], low), NZ, 1)

    def level_pass(planes, st, body, staged=True, field=None, e=None, out_st=None):
        lane, row = lane_ids(), row_ids()
        out_st = st if out_st is None else out_st
        spot = ((lane + out_st) % NZ) // (2 * out_st)
        if e is not None:
            beyond = jnp.where((lane // st) % 2 == 0, hz[e, 1], pltpu.roll(hz[e, 0], 2 * st, 1))

        def step(g, packed):
            xs = [g * GROUP + i for i in range(GROUP)]
            hoods = [None] * GROUP
            if e is not None:
                loaded = [field[xs[0] + i] for i in range(GROUP + 2)]
                hoods = []
                for i in range(GROUP):
                    c = loaded[i + 1]
                    yl = jnp.where(row < st, hy[e, 0, pl.ds(xs[i], 1), :], pltpu.roll(c, st, 0))
                    yh = jnp.where(row >= NY - st, hy[e, 1, pl.ds(xs[i], 1), :], pltpu.roll(c, NY - st, 0))
                    w = pltpu.roll(beyond, (LANES + NZ - st - xs[i] * (2 * st)) % LANES, 1)
                    zl = jnp.where(lane % NZ < st, w, pltpu.roll(c, st, 1))
                    zh = jnp.where(lane % NZ >= NZ - st, w, pltpu.roll(c, LANES - st, 1))
                    hoods.append((c, loaded[i], loaded[i + 2], yl, yh, zl, zh))
            results = body(xs, hoods)
            if staged:
                places = [g * len(results) + i for i in range(len(results))]
                for x, n in zip(places, results):
                    packed = jnp.where(spot == x, pltpu.roll(n, x * (2 * out_st), 1), packed)
                for x, n in zip(places, results):
                    ys[0, pl.ds(x, 1), :] = n[0:1, :]
                    ys[1, pl.ds(x, 1), :] = n[NY - 1:NY, :]
            return packed

        if staged:
            zs[...] = lax.fori_loop(0, planes // GROUP, step, jnp.zeros((NY, LANES), F32))
        else:
            lax.fori_loop(0, planes // GROUP, step, 0)

    def fine_nb(x, hood):
        c, xl, xh, yl, yh, zl, zh = hood
        return c, (
            (fx[x] * xl + fx[x + 1] * xh) + (fyl[x] * yl + fyh[x] * yh) + (fzl[x] * zl + fzh[x] * zh)
        )

    def coarse_nb(x, hood):
        c, xl, xh, yl, yh, zl, zh = hood
        return c, (
            (cfx[x] * xl + cfx[x + 1] * xh) + (cfyl[x] * yl + cfyh[x] * yh) + (cfzl[x] * zl + cfzh[x] * zh)
        )

    def is_colour(x, st, colour):
        return (row_ids() // st + lane_ids() // st + x + colour) % 2 == 0

    forward(0)
    send_pieces(2)
    forward(1)
    unpack(0, bv, 1)
    level_pass(PLANES, 1, lambda xs, hoods: [bv[x + 1] for x in xs])
    exchange(0, bv, PLANES, ("start",))
    forward(2)
    exchange(0, bv, PLANES, ("wait",))

    def faces(xs, hoods):
        for x, (c, xl, xh, yl, yh, zl, zh) in zip(xs, hoods):
            fx[x] = 0.5 * (c + xl)
            fyl[x] = 0.5 * (c + yl)
            fyh[x] = 0.5 * (c + yh)
            fzl[x] = 0.5 * (c + zl)
            fzh[x] = 0.5 * (c + zh)

    level_pass(PLANES, 1, faces, staged=False, field=bv, e=0)
    fx[PLANES] = 0.5 * (bv[PLANES] + bv[PLANES + 1])

    unpack(1, ac, 0)

    @pl.loop(0, PLANES // 2)
    def _(i):
        x = 2 * i
        for o in range(2):
            d = ac[x + o] + (
                (fx[x + o] + fx[x + o + 1]) + (fyl[x + o] + fyh[x + o]) + (fzl[x + o] + fzh[x + o])
            )
            dg[x + o] = d
            rd[x + o] = 1.0 / d
        s = 0.0625
        wxl = s * pair_z(pair_y(fx[x]))
        wxh = s * pair_z(pair_y(fx[x + 2]))
        wyl = s * pair_z(even_y(fyl[x] + fyl[x + 1]))
        wyh = s * pair_z(odd_y(fyh[x] + fyh[x + 1]))
        wzl = s * pair_y(even_z(fzl[x] + fzl[x + 1]))
        wzh = s * pair_y(odd_z(fzh[x] + fzh[x + 1]))
        cfx[i] = wxl
        cfx[i + 1] = wxh
        cfyl[i] = wyl
        cfyh[i] = wyh
        cfzl[i] = wzl
        cfzh[i] = wzh
        ca = 0.125 * pair_z(pair_y(ac[x] + ac[x + 1]))
        crd[i] = 1.0 / (ca + ((wxl + wxh) + (wyl + wyh) + (wzl + wzh)))

    unpack(2, rh, 0)

    def store(field, xs, values):
        for x, n in zip(xs, values):
            field[x + 1] = n
        return values

    def first_red(xs, hoods):
        return store(v, xs, [jnp.where(is_colour(x, 1, 0), rh[x] * rd[x], 0.0) for x in xs])

    def half(e, colour):
        def update(xs, hoods):
            values = []
            for x, hood in zip(xs, hoods):
                c, nb = fine_nb(x, hood)
                values.append(jnp.where(is_colour(x, 1, colour), (rh[x] + nb) * rd[x], c))
            return store(v, xs, values)

        level_pass(PLANES, 1, update, field=v, e=e)

    level_pass(PLANES, 1, first_red)
    exchange(1, v, PLANES)
    half(1, 1)
    exchange(2, v, PLANES)

    def restrict(xs, hoods):
        values = []
        for p in range(0, GROUP, 2):
            total = None
            for x, hood in zip(xs[p:p + 2], hoods[p:p + 2]):
                c, nb = fine_nb(x, hood)
                r = rh[x] - (dg[x] * c - nb)
                total = r if total is None else total + r
            values.append(0.125 * pair_z(pair_y(total)))
        places = [xs[0] // 2 + i for i in range(GROUP // 2)]
        for i, f in zip(places, values):
            cf[i] = f
        return store(
            cc, places,
            [jnp.where(is_colour(i, 2, 0), f * crd[i], 0.0) for i, f in zip(places, values)],
        )

    level_pass(PLANES, 1, restrict, field=v, e=2, out_st=2)

    def coarse_half(h, xs, hoods):
        values = []
        for x, hood in zip(xs, hoods):
            c, nb = coarse_nb(x, hood)
            values.append(jnp.where(is_colour(x, 2, h), (cf[x] + nb) * crd[x], c))
        return values

    @pl.loop(1, COARSE_HALVES - 1)
    def _(h):
        exchange(2 + h, cc, PLANES // 2)
        level_pass(
            PLANES // 2, 2, lambda xs, hoods: store(cc, xs, coarse_half(h, xs, hoods)),
            field=cc, e=2 + h,
        )

    def correct(xs, hoods):
        values = []
        for x, n in zip(xs, coarse_half(COARSE_HALVES - 1, xs, hoods)):
            values += [v[2 * x + 1] + n, v[2 * x + 2] + n]
        return store(v, [2 * xs[0] + i for i in range(2 * GROUP)], values)

    exchange(9, cc, PLANES // 2)
    level_pass(PLANES // 2, 2, correct, field=cc, e=9, out_st=1)
    exchange(10, v, PLANES)
    half(10, 0)
    exchange(11, v, PLANES)
    half(11, 1)
    exchange(12, v, PLANES)

    def finish(xs, hoods):
        for x, hood in zip(xs, hoods):
            c, nb = fine_nb(x, hood)
            r = rh[x] - (dg[x] * c - nb)
            for out, n in ((sol_out, c), (res_out, r)):
                out[x] = n[:, :NZ]
                out[x + PLANES] = pltpu.roll(n, NZ, 1)[:, :NZ]

    level_pass(PLANES, 1, finish, staged=False, field=v, e=12)

    @pl.loop(1, members)
    def _(k):
        peer = partner(k)
        place_copy(peer, k, me).wait_send()
        for f in range(3):
            copy1(f, peer, k, me).wait_send()
            copy2(f, peer, k, me).wait_send()


def solution(mesh):
    sizes = (mesh.shape["gx"], mesh.shape["gy"], mesh.shape["gz"])
    members = sizes[0] * sizes[1]
    rows = 256 // members

    def rows128(boxes):
        return boxes[0].reshape(4, 256, LANES).transpose(1, 0, 2).reshape(1024, LANES)

    def body(rhs_boxes, a_boxes, b_boxes, new_place):
        spot = jnp.where(jnp.arange(8)[:, None] < 4, jnp.tile(new_place[0], 2)[:, None], -1)
        spot = jnp.broadcast_to(spot, (8, LANES)).astype(jnp.int32)
        fine = pltpu.VMEM((PLANES, NY, LANES), F32)
        coarse = pltpu.VMEM((PLANES // 2, NY, LANES), F32)
        box = pltpu.VMEM((members, 4 * rows, LANES), F32)
        boxes = pltpu.VMEM((3, members, 4 * rows, LANES), F32)
        dma = pltpu.SemaphoreType.DMA
        return pl.pallas_call(
            functools.partial(kernel, sizes),
            out_shape=[jax.ShapeDtypeStruct((NX, NY, NZ), F32)] * 2,
            in_specs=[pl.BlockSpec(memory_space=pltpu.VMEM)] + [pl.BlockSpec(memory_space=pltpu.HBM)] * 3,
            out_specs=[pl.BlockSpec(memory_space=pltpu.VMEM)] * 2,
            scratch_shapes=[
                pltpu.VMEM((members, 8, LANES), jnp.int32),
                pltpu.VMEM((8, LANES), jnp.int32),
                pltpu.SMEM((8, LANES), jnp.int32),
                box, box, box, boxes, boxes,
                pltpu.VMEM((PLANES + 2, NY, LANES), F32),
                fine, fine, fine, fine,
                pltpu.VMEM((PLANES + 1, NY, LANES), F32),
                fine, fine, fine, fine,
                pltpu.VMEM((PLANES + 2, NY, LANES), F32),
                pltpu.VMEM((PLANES // 2 + 2, NY, LANES), F32),
                coarse, coarse,
                pltpu.VMEM((PLANES // 2 + 1, NY, LANES), F32),
                coarse, coarse, coarse, coarse,
                pltpu.VMEM((EXCHANGES, 2, NY, LANES), F32),
                pltpu.VMEM((EXCHANGES, 2, PLANES, LANES), F32),
                pltpu.VMEM((EXCHANGES, 2, NY, LANES), F32),
                pltpu.VMEM((2, PLANES, LANES), F32),
                pltpu.VMEM((NY, LANES), F32),
                dma((members,)), dma((members,)),
                dma((3, members)), dma((3, members)),
                dma((3, members)), dma((3, members)),
                dma,
                dma((6,)), dma((EXCHANGES, 6)),
            ],
            compiler_params=pltpu.CompilerParams(
                collective_id=0, has_side_effects=True, vmem_limit_bytes=60 * 1024 * 1024
            ),
        )(spot, rows128(rhs_boxes), rows128(a_boxes), rows128(b_boxes))

    return jax.shard_map(
        body,
        mesh=mesh,
        in_specs=(
            P("gz", ("gx", "gy"), None),
            P("gz", ("gx", "gy"), None),
            P("gz", ("gx", "gy"), None),
            P("gz", ("gx", "gy")),
        ),
        out_specs=(P("gx", "gy", "gz"), P("gx", "gy", "gz")),
        check_vma=False,
    )
```

```python
import functools

import jax
import jax.numpy as jnp
from jax import lax
from jax.experimental import pallas as pl
from jax.experimental.pallas import tpu as pltpu
from jax.sharding import PartitionSpec as P

MESH = pl.DeviceIdType.MESH
NX, NY, NZ = 64, 32, 64
PLANES = NX // 2
LANES = 128
COARSE_HALVES = 8
EXCHANGES = 13
GROUP = 8
F32 = jnp.float32


def lane_ids():
    return lax.broadcasted_iota(jnp.int32, (NY, LANES), 1)


def row_ids():
    return lax.broadcasted_iota(jnp.int32, (NY, LANES), 0)


def pair_z(v):
    return v + jnp.where(lane_ids() % 2 == 0, pltpu.roll(v, LANES - 1, 1), pltpu.roll(v, 1, 1))


def pair_y(v):
    return v + jnp.where(row_ids() % 2 == 0, pltpu.roll(v, NY - 1, 0), pltpu.roll(v, 1, 0))


def even_y(v):
    return jnp.where(row_ids() % 2 == 0, v, pltpu.roll(v, 1, 0))


def odd_y(v):
    return jnp.where(row_ids() % 2 == 1, v, pltpu.roll(v, NY - 1, 0))


def even_z(v):
    return jnp.where(lane_ids() % 2 == 0, v, pltpu.roll(v, 1, 1))


def odd_z(v):
    return jnp.where(lane_ids() % 2 == 1, v, pltpu.roll(v, LANES - 1, 1))


def kernel(
    sizes,
    place_ref, rhs_in, a_in, b_in,
    sol_out, res_out,
    got_place, inv_vmem, inv_smem, got_b, got_a, got_rhs, sorted_, final,
    bv, rh, ac, dg, rd, fx, fyl, fyh, fzl, fzh, v,
    cc, cf, crd, cfx, cfyl, cfyh, cfzl, cfzh,
    fye, fze, cfye, cfze, inner,
    hx, hy, hz, ys, zs,
    place_send, place_recv, send1, recv1, send2, recv2, inv_sem, halo_send, halo_recv,
):
    n_gx, n_gy, n_gz = sizes
    members = n_gx * n_gy
    rows = 256 // members
    slabs = rows // 8
    gx, gy, gz = lax.axis_index("gx"), lax.axis_index("gy"), lax.axis_index("gz")
    me = gx * n_gy + gy
    got = (got_b, got_a, got_rhs)

    def partner(k):
        return (me + 1 + (k + members // 2 - 2) % (members - 1)) % members

    def sender(k):
        return (me + members - 1 - (k + members // 2 - 2) % (members - 1)) % members

    def member(t):
        return (t // n_gy, t % n_gy, gz)

    @pl.loop(0, EXCHANGES)
    def _(e):
        for side in range(2):
            hx[e, side] = jnp.zeros((NY, LANES), F32)
            hy[e, side] = jnp.zeros((PLANES, LANES), F32)
            hz[e, side] = jnp.zeros((NY, LANES), F32)

    barrier = pltpu.get_barrier_semaphore()

    @pl.loop(1, members)
    def _(k):
        pl.semaphore_signal(barrier, inc=1, device_id=member((me + k) % members), device_id_type=MESH)

    @pl.when(gz > 0)
    def _():
        pl.semaphore_signal(barrier, inc=1, device_id=(gx, gy, gz - 1), device_id_type=MESH)

    @pl.when(gz < n_gz - 1)
    def _():
        pl.semaphore_signal(barrier, inc=1, device_id=(gx, gy, gz + 1), device_id_type=MESH)

    pl.semaphore_wait(
        barrier, members - 1 + (gz > 0).astype(jnp.int32) + (gz < n_gz - 1).astype(jnp.int32)
    )

    def place_copy(peer, k, slot):
        return pltpu.make_async_remote_copy(
            src_ref=place_ref, dst_ref=got_place.at[slot],
            send_sem=place_send.at[k], recv_sem=place_recv.at[slot],
            device_id=member(peer), device_id_type=MESH,
        )

    def copy1(f, peer, k, slot):
        return pltpu.make_async_remote_copy(
            src_ref=(b_in, a_in, rhs_in)[f].at[pl.ds(pl.multiple_of(peer * 4 * rows, 8), 4 * rows)],
            dst_ref=got[f].at[slot],
            send_sem=send1.at[f, k], recv_sem=recv1.at[f, slot],
            device_id=member(peer), device_id_type=MESH,
        )

    def copy2(f, peer, k, slot):
        return pltpu.make_async_remote_copy(
            src_ref=sorted_.at[f, peer], dst_ref=final.at[f, slot],
            send_sem=send2.at[f, k], recv_sem=recv2.at[f, slot],
            device_id=member(peer), device_id_type=MESH,
        )

    @pl.loop(1, members)
    def _(k):
        place_copy(partner(k), k, me).start()

    def own1(f):
        return pltpu.make_async_copy(
            (b_in, a_in, rhs_in)[f].at[pl.ds(pl.multiple_of(me * 4 * rows, 8), 4 * rows)],
            got[f].at[me], recv1.at[f, me],
        )

    def send_pieces(f):
        own1(f).start()

        @pl.loop(1, members)
        def _(k):
            copy1(f, partner(k), k, me).start()

    send_pieces(0)
    send_pieces(1)
    got_place[me] = place_ref[...]

    @pl.loop(1, members)
    def _(k):
        place_copy((me + k) % members, k, (me + k) % members).wait_recv()

    lane8 = lax.broadcasted_iota(jnp.int32, (8, LANES), 1)
    row8 = lax.broadcasted_iota(jnp.int32, (8, LANES), 0)

    def find(src, total):
        here = (got_place[src] == lane8) & (row8 < 4)
        return jnp.maximum(total, jnp.where(here, src * 4 + row8, 0))

    owner = lax.fori_loop(0, members, find, jnp.zeros((8, LANES), jnp.int32))
    for shift in (4, 2, 1):
        owner = jnp.maximum(owner, pltpu.roll(owner, shift, 0))
    inv_vmem[...] = owner
    inv_copy = pltpu.make_async_copy(inv_vmem, inv_smem, inv_sem)
    inv_copy.start()
    inv_copy.wait()

    def forward(f):
        own1(f).wait()

        @pl.loop(1, members)
        def _(k):
            copy1(f, (me + k) % members, k, (me + k) % members).wait_recv()

        def pick(t, q):
            index = inv_smem[0, t * 4 + q]
            return got[f][index >> 2, pl.ds(index & 3, rows, stride=4), :]

        @pl.loop(1, members)
        def _(k):
            t = partner(k)
            for q in range(4):
                sorted_[f, t, q * rows:(q + 1) * rows, :] = pick(t, q)
            copy2(f, t, k, me).start()

        for q in range(4):
            final[f, me, q * rows:(q + 1) * rows, :] = pick(me, q)

    def unpack(f, out, first):
        def one(j):
            for slab in range(slabs):
                tiles = [final[f, j, q * rows + slab * 8:q * rows + slab * 8 + 8, :] for q in range(4)]
                for yr in range(4):
                    whole = tiles[yr]
                    for q in range(4):
                        if q != yr:
                            turned = pltpu.roll(tiles[q], (32 * (q - yr)) % LANES, 1)
                            whole = jnp.where(lane8 // 32 == q, turned, whole)
                    out[j * slabs + slab + first, pl.ds(yr, 8, stride=4), :] = whole

        one(me)

        @pl.loop(1, members)
        def _(k):
            j = sender(k)
            copy2(f, j, k, j).wait_recv()
            one(j)

    def exchange(e, field, planes, acts=("start", "wait")):
        for act in acts:
            if act == "only":
                continue
            for axis in (1, 0, 2):
                for side in range(2):
                    d = axis * 2 + side
                    place, count = ((gx, n_gx), (gy, n_gy), (gz, n_gz))[axis]
                    there = place > 0 if side == 0 else place < count - 1
                    other = [gx, gy, gz]
                    other[axis] = place + (2 * side - 1)
                    if axis == 0:
                        src, dst = field.at[1 if side == 0 else planes], hx
                        to, mine = dst.at[e, 1 - side], dst.at[e, side]
                    elif axis == 1:
                        src = ys.at[side, pl.ds(0, planes)]
                        to, mine = hy.at[e, 1 - side, pl.ds(0, planes)], hy.at[e, side, pl.ds(0, planes)]
                    else:
                        src, to, mine = zs, hz.at[e, 1 - side], hz.at[e, side]

                    @pl.when(there)
                    def _():
                        out = pltpu.make_async_remote_copy(
                            src_ref=src, dst_ref=to, send_sem=halo_send.at[d],
                            recv_sem=halo_recv.at[e, axis * 2 + 1 - side],
                            device_id=tuple(other), device_id_type=MESH,
                        )
                        if act == "start":
                            out.start()
                        else:
                            out.wait_send()
                            pltpu.make_async_remote_copy(
                                src_ref=src, dst_ref=mine, send_sem=halo_send.at[d],
                                recv_sem=halo_recv.at[e, d],
                                device_id=tuple(other), device_id_type=MESH,
                            ).wait_recv()
        if acts[-1] != "wait":
            return
        low, lane = field[1], lane_ids()
        field[0] = pltpu.roll(jnp.where(lane >= NZ, hx[e, 0], field[planes]), NZ, 1)
        field[planes + 1] = pltpu.roll(jnp.where(lane < NZ, hx[e, 1], low), NZ, 1)

    def level_pass(planes, st, body, staged=True, field=None, e=None, out_st=None):
        lane, row = lane_ids(), row_ids()
        out_st = st if out_st is None else out_st
        spot = ((lane + out_st) % NZ) // (2 * out_st)
        if e is not None:
            beyond = jnp.where((lane // st) % 2 == 0, hz[e, 1], pltpu.roll(hz[e, 0], 2 * st, 1))

        def step(g, packed):
            xs = [g * GROUP + i for i in range(GROUP)]
            hoods = [None] * GROUP
            if e is not None:
                loaded = [field[xs[0] + i] for i in range(GROUP + 2)]
                hoods = []
                for i in range(GROUP):
                    c = loaded[i + 1]
                    yl = jnp.where(row < st, hy[e, 0, pl.ds(xs[i], 1), :], pltpu.roll(c, st, 0))
                    yh = jnp.where(row >= NY - st, hy[e, 1, pl.ds(xs[i], 1), :], pltpu.roll(c, NY - st, 0))
                    w = pltpu.roll(beyond, (LANES + NZ - st - xs[i] * (2 * st)) % LANES, 1)
                    zl = jnp.where(lane % NZ < st, w, pltpu.roll(c, st, 1))
                    zh = jnp.where(lane % NZ >= NZ - st, w, pltpu.roll(c, LANES - st, 1))
                    hoods.append((c, loaded[i], loaded[i + 2], yl, yh, zl, zh))
            results = body(xs, hoods)
            if staged:
                places = [g * len(results) + i for i in range(len(results))]
                for x, n in zip(places, results):
                    packed = jnp.where(spot == x, pltpu.roll(n, x * (2 * out_st), 1), packed)
                for x, n in zip(places, results):
                    ys[0, pl.ds(x, 1), :] = n[0:1, :]
                    ys[1, pl.ds(x, 1), :] = n[NY - 1:NY, :]
            return packed

        if staged:
            zs[...] = lax.fori_loop(0, planes // GROUP, step, jnp.zeros((NY, LANES), F32))
        else:
            lax.fori_loop(0, planes // GROUP, step, 0)

    fine_faces = (fx, fyl, fyh, fzl, fzh, fye, fze)
    coarse_faces = (cfx, cfyl, cfyh, cfzl, cfzh, cfye, cfze)

    def split_faces(st, yl, yh, zl, zh):
        row, z = row_ids(), lane_ids() % NZ
        y_low, y_high, z_low, z_high = row < st, row >= NY - st, z < st, z >= NZ - st
        return (
            jnp.where(y_low, 0.0, yl), jnp.where(y_high, 0.0, yh),
            jnp.where(z_low, 0.0, zl), jnp.where(z_high, 0.0, zh),
            jnp.where(y_low, yl, jnp.where(y_high, yh, 0.0)),
            jnp.where(z_low, zl, jnp.where(z_high, zh, 0.0)),
        )

    def halo_pass(field, e, planes, st, faces, body, staged=True, out_st=None):
        across, yl, yh, zl, zh, ye, ze = faces
        exchange(e, field, planes, ("start",))
        lane = lane_ids()
        first, last = field[1], field[planes]
        field[0] = pltpu.roll(jnp.where(lane < NZ, last, 0.0), NZ, 1)
        field[planes + 1] = pltpu.roll(jnp.where(lane >= NZ, first, 0.0), NZ, 1)

        @pl.loop(0, planes // GROUP)
        def _(g):
            xs = [g * GROUP + i for i in range(GROUP)]
            loaded = [field[xs[0] + i] for i in range(GROUP + 2)]
            sums = []
            for i, x in enumerate(xs):
                c = loaded[i + 1]
                sums.append(
                    (across[x] * loaded[i] + across[x + 1] * loaded[i + 2])
                    + (yl[x] * pltpu.roll(c, st, 0) + yh[x] * pltpu.roll(c, NY - st, 0))
                    + (zl[x] * pltpu.roll(c, st, 1) + zh[x] * pltpu.roll(c, LANES - st, 1))
                )
            for x, total in zip(xs, sums):
                inner[x] = total

        exchange(e, field, planes, ("wait", "only"))
        inner[0] += across[0] * pltpu.roll(jnp.where(lane >= NZ, hx[e, 0], 0.0), NZ, 1)
        inner[planes - 1] += across[planes] * pltpu.roll(jnp.where(lane < NZ, hx[e, 1], 0.0), NZ, 1)
        beyond = jnp.where((lane // st) % 2 == 0, hz[e, 1], pltpu.roll(hz[e, 0], 2 * st, 1))
        lower = row_ids() < NY // 2

        def with_halos(xs, hoods):
            pairs = []
            for x in xs:
                w = pltpu.roll(beyond, (LANES + NZ - st - x * (2 * st)) % LANES, 1)
                y = jnp.where(lower, hy[e, 0, pl.ds(x, 1), :], hy[e, 1, pl.ds(x, 1), :])
                pairs.append((field[x + 1], inner[x] + (ye[x] * y + ze[x] * w)))
            return body(xs, pairs)

        level_pass(planes, st, with_halos, staged=staged, out_st=out_st)

    def is_colour(x, st, colour):
        return (row_ids() // st + lane_ids() // st + x + colour) % 2 == 0

    forward(0)
    send_pieces(2)
    forward(1)
    unpack(0, bv, 1)
    level_pass(PLANES, 1, lambda xs, hoods: [bv[x + 1] for x in xs])
    exchange(0, bv, PLANES, ("start",))
    forward(2)
    exchange(0, bv, PLANES, ("wait",))

    def faces(xs, hoods):
        for x, (c, xl, xh, yl, yh, zl, zh) in zip(xs, hoods):
            fx[x] = 0.5 * (c + xl)
            fyl[x] = 0.5 * (c + yl)
            fyh[x] = 0.5 * (c + yh)
            fzl[x] = 0.5 * (c + zl)
            fzh[x] = 0.5 * (c + zh)

    level_pass(PLANES, 1, faces, staged=False, field=bv, e=0)
    fx[PLANES] = 0.5 * (bv[PLANES] + bv[PLANES + 1])

    unpack(1, ac, 0)

    @pl.loop(0, PLANES // 2)
    def _(i):
        x = 2 * i
        for o in range(2):
            d = ac[x + o] + (
                (fx[x + o] + fx[x + o + 1]) + (fyl[x + o] + fyh[x + o]) + (fzl[x + o] + fzh[x + o])
            )
            dg[x + o] = d
            rd[x + o] = 1.0 / d
        s = 0.0625
        wxl = s * pair_z(pair_y(fx[x]))
        wxh = s * pair_z(pair_y(fx[x + 2]))
        wyl = s * pair_z(even_y(fyl[x] + fyl[x + 1]))
        wyh = s * pair_z(odd_y(fyh[x] + fyh[x + 1]))
        wzl = s * pair_y(even_z(fzl[x] + fzl[x + 1]))
        wzh = s * pair_y(odd_z(fzh[x] + fzh[x + 1]))
        cfx[i] = wxl
        cfx[i + 1] = wxh
        for ref, face in zip(coarse_faces[1:], split_faces(2, wyl, wyh, wzl, wzh)):
            ref[i] = face
        ca = 0.125 * pair_z(pair_y(ac[x] + ac[x + 1]))
        crd[i] = 1.0 / (ca + ((wxl + wxh) + (wyl + wyh) + (wzl + wzh)))
        for o in range(2):
            full = split_faces(1, fyl[x + o], fyh[x + o], fzl[x + o], fzh[x + o])
            for ref, face in zip(fine_faces[1:], full):
                ref[x + o] = face

    unpack(2, rh, 0)

    def store(field, xs, values):
        for x, n in zip(xs, values):
            field[x + 1] = n
        return values

    def first_red(xs, hoods):
        return store(v, xs, [jnp.where(is_colour(x, 1, 0), rh[x] * rd[x], 0.0) for x in xs])

    def half(e, colour):
        def update(xs, hoods):
            values = []
            for x, hood in zip(xs, hoods):
                c, nb = hood
                values.append(jnp.where(is_colour(x, 1, colour), (rh[x] + nb) * rd[x], c))
            return store(v, xs, values)

        halo_pass(v, e, PLANES, 1, fine_faces, update)

    level_pass(PLANES, 1, first_red)
    half(1, 1)

    def restrict(xs, hoods):
        values = []
        for p in range(0, GROUP, 2):
            total = None
            for x, hood in zip(xs[p:p + 2], hoods[p:p + 2]):
                c, nb = hood
                r = rh[x] - (dg[x] * c - nb)
                total = r if total is None else total + r
            values.append(0.125 * pair_z(pair_y(total)))
        places = [xs[0] // 2 + i for i in range(GROUP // 2)]
        for i, f in zip(places, values):
            cf[i] = f
        return store(
            cc, places,
            [jnp.where(is_colour(i, 2, 0), f * crd[i], 0.0) for i, f in zip(places, values)],
        )

    halo_pass(v, 2, PLANES, 1, fine_faces, restrict, out_st=2)

    def coarse_half(h, xs, hoods):
        values = []
        for x, hood in zip(xs, hoods):
            c, nb = hood
            values.append(jnp.where(is_colour(x, 2, h), (cf[x] + nb) * crd[x], c))
        return values

    @pl.loop(1, COARSE_HALVES - 1)
    def _(h):
        halo_pass(
            cc, 2 + h, PLANES // 2, 2, coarse_faces,
            lambda xs, hoods: store(cc, xs, coarse_half(h, xs, hoods)),
        )

    def correct(xs, hoods):
        values = []
        for x, n in zip(xs, coarse_half(COARSE_HALVES - 1, xs, hoods)):
            values += [v[2 * x + 1] + n, v[2 * x + 2] + n]
        return store(v, [2 * xs[0] + i for i in range(2 * GROUP)], values)

    halo_pass(cc, 9, PLANES // 2, 2, coarse_faces, correct, out_st=1)
    half(10, 0)
    half(11, 1)

    def finish(xs, hoods):
        for x, hood in zip(xs, hoods):
            c, nb = hood
            r = rh[x] - (dg[x] * c - nb)
            for out, n in ((sol_out, c), (res_out, r)):
                out[x] = n[:, :NZ]
                out[x + PLANES] = pltpu.roll(n, NZ, 1)[:, :NZ]

    halo_pass(v, 12, PLANES, 1, fine_faces, finish, staged=False)

    @pl.loop(1, members)
    def _(k):
        peer = partner(k)
        place_copy(peer, k, me).wait_send()
        for f in range(3):
            copy1(f, peer, k, me).wait_send()
            copy2(f, peer, k, me).wait_send()


def solution(mesh):
    sizes = (mesh.shape["gx"], mesh.shape["gy"], mesh.shape["gz"])
    members = sizes[0] * sizes[1]
    rows = 256 // members

    def rows128(boxes):
        return boxes[0].reshape(4, 256, LANES).transpose(1, 0, 2).reshape(1024, LANES)

    def body(rhs_boxes, a_boxes, b_boxes, new_place):
        spot = jnp.where(jnp.arange(8)[:, None] < 4, jnp.tile(new_place[0], 2)[:, None], -1)
        spot = jnp.broadcast_to(spot, (8, LANES)).astype(jnp.int32)
        fine = pltpu.VMEM((PLANES, NY, LANES), F32)
        coarse = pltpu.VMEM((PLANES // 2, NY, LANES), F32)
        box = pltpu.VMEM((members, 4 * rows, LANES), F32)
        boxes = pltpu.VMEM((3, members, 4 * rows, LANES), F32)
        dma = pltpu.SemaphoreType.DMA
        return pl.pallas_call(
            functools.partial(kernel, sizes),
            out_shape=[jax.ShapeDtypeStruct((NX, NY, NZ), F32)] * 2,
            in_specs=[pl.BlockSpec(memory_space=pltpu.VMEM)] + [pl.BlockSpec(memory_space=pltpu.HBM)] * 3,
            out_specs=[pl.BlockSpec(memory_space=pltpu.VMEM)] * 2,
            scratch_shapes=[
                pltpu.VMEM((members, 8, LANES), jnp.int32),
                pltpu.VMEM((8, LANES), jnp.int32),
                pltpu.SMEM((8, LANES), jnp.int32),
                box, box, box, boxes, boxes,
                pltpu.VMEM((PLANES + 2, NY, LANES), F32),
                fine, fine, fine, fine,
                pltpu.VMEM((PLANES + 1, NY, LANES), F32),
                fine, fine, fine, fine,
                pltpu.VMEM((PLANES + 2, NY, LANES), F32),
                pltpu.VMEM((PLANES // 2 + 2, NY, LANES), F32),
                coarse, coarse,
                pltpu.VMEM((PLANES // 2 + 1, NY, LANES), F32),
                coarse, coarse, coarse, coarse,
                fine, fine, coarse, coarse, fine,
                pltpu.VMEM((EXCHANGES, 2, NY, LANES), F32),
                pltpu.VMEM((EXCHANGES, 2, PLANES, LANES), F32),
                pltpu.VMEM((EXCHANGES, 2, NY, LANES), F32),
                pltpu.VMEM((2, PLANES, LANES), F32),
                pltpu.VMEM((NY, LANES), F32),
                dma((members,)), dma((members,)),
                dma((3, members)), dma((3, members)),
                dma((3, members)), dma((3, members)),
                dma,
                dma((6,)), dma((EXCHANGES, 6)),
            ],
            compiler_params=pltpu.CompilerParams(
                collective_id=0, has_side_effects=True, vmem_limit_bytes=60 * 1024 * 1024
            ),
        )(spot, rows128(rhs_boxes), rows128(a_boxes), rows128(b_boxes))

    return jax.shard_map(
        body,
        mesh=mesh,
        in_specs=(
            P("gz", ("gx", "gy"), None),
            P("gz", ("gx", "gy"), None),
            P("gz", ("gx", "gy"), None),
            P("gz", ("gx", "gy")),
        ),
        out_specs=(P("gx", "gy", "gz"), P("gx", "gy", "gz")),
        check_vma=False,
    )
```

```python
import functools

import jax
import jax.numpy as jnp
from jax import lax
from jax.experimental import pallas as pl
from jax.experimental.pallas import tpu as pltpu
from jax.sharding import PartitionSpec as P

MESH = pl.DeviceIdType.MESH
NX, NY, NZ = 64, 32, 64
PLANES = NX // 2
LANES = 128
COARSE_HALVES = 8
EXCHANGES = 13
GROUP = 8
F32 = jnp.float32


def lane_ids():
    return lax.broadcasted_iota(jnp.int32, (NY, LANES), 1)


def row_ids():
    return lax.broadcasted_iota(jnp.int32, (NY, LANES), 0)


def pair_z(v):
    return v + jnp.where(lane_ids() % 2 == 0, pltpu.roll(v, LANES - 1, 1), pltpu.roll(v, 1, 1))


def pair_y(v):
    return v + jnp.where(row_ids() % 2 == 0, pltpu.roll(v, NY - 1, 0), pltpu.roll(v, 1, 0))


def even_y(v):
    return jnp.where(row_ids() % 2 == 0, v, pltpu.roll(v, 1, 0))


def odd_y(v):
    return jnp.where(row_ids() % 2 == 1, v, pltpu.roll(v, NY - 1, 0))


def even_z(v):
    return jnp.where(lane_ids() % 2 == 0, v, pltpu.roll(v, 1, 1))


def odd_z(v):
    return jnp.where(lane_ids() % 2 == 1, v, pltpu.roll(v, LANES - 1, 1))


def kernel(
    sizes,
    place_ref, rhs_in, a_in, b_in,
    sol_out, res_out,
    got_place, inv_vmem, inv_smem, got_b, got_a, got_rhs, sorted_, final,
    bv, rh, ac, dg, rd, fx, fyl, fyh, fzl, fzh, v,
    cc, cf, crd, cfx, cfyl, cfyh, cfzl, cfzh,
    fye, fze, cfye, cfze, inner,
    hx, hy, hz, ys, zs,
    place_send, place_recv, send1, recv1, send2, recv2, inv_sem, halo_send, halo_recv,
):
    n_gx, n_gy, n_gz = sizes
    members = n_gx * n_gy
    rows = 256 // members
    slabs = rows // 8
    gx, gy, gz = lax.axis_index("gx"), lax.axis_index("gy"), lax.axis_index("gz")
    me = gx * n_gy + gy
    got = (got_b, got_a, got_rhs)

    def partner(k):
        return (me + 1 + (k + members // 2 - 2) % (members - 1)) % members

    def sender(k):
        return (me + members - 1 - (k + members // 2 - 2) % (members - 1)) % members

    def member(t):
        return (t // n_gy, t % n_gy, gz)

    @pl.loop(0, EXCHANGES)
    def _(e):
        for side in range(2):
            hx[e, side] = jnp.zeros((NY, LANES), F32)
            hy[e, side] = jnp.zeros((PLANES, LANES), F32)
            hz[e, side] = jnp.zeros((NY, LANES), F32)

    barrier = pltpu.get_barrier_semaphore()

    @pl.loop(1, members)
    def _(k):
        pl.semaphore_signal(barrier, inc=1, device_id=member((me + k) % members), device_id_type=MESH)

    @pl.when(gz > 0)
    def _():
        pl.semaphore_signal(barrier, inc=1, device_id=(gx, gy, gz - 1), device_id_type=MESH)

    @pl.when(gz < n_gz - 1)
    def _():
        pl.semaphore_signal(barrier, inc=1, device_id=(gx, gy, gz + 1), device_id_type=MESH)

    pl.semaphore_wait(
        barrier, members - 1 + (gz > 0).astype(jnp.int32) + (gz < n_gz - 1).astype(jnp.int32)
    )

    def place_copy(peer, k, slot):
        return pltpu.make_async_remote_copy(
            src_ref=place_ref, dst_ref=got_place.at[slot],
            send_sem=place_send.at[k], recv_sem=place_recv.at[slot],
            device_id=member(peer), device_id_type=MESH,
        )

    def copy1(f, peer, k, slot):
        return pltpu.make_async_remote_copy(
            src_ref=(b_in, a_in, rhs_in)[f].at[pl.ds(pl.multiple_of(peer * 4 * rows, 8), 4 * rows)],
            dst_ref=got[f].at[slot],
            send_sem=send1.at[f, k], recv_sem=recv1.at[f, slot],
            device_id=member(peer), device_id_type=MESH,
        )

    def copy2(f, peer, k, slot):
        return pltpu.make_async_remote_copy(
            src_ref=sorted_.at[f, peer], dst_ref=final.at[f, slot],
            send_sem=send2.at[f, k], recv_sem=recv2.at[f, slot],
            device_id=member(peer), device_id_type=MESH,
        )

    @pl.loop(1, members)
    def _(k):
        place_copy(partner(k), k, me).start()

    def own1(f):
        return pltpu.make_async_copy(
            (b_in, a_in, rhs_in)[f].at[pl.ds(pl.multiple_of(me * 4 * rows, 8), 4 * rows)],
            got[f].at[me], recv1.at[f, me],
        )

    def send_pieces(f):
        own1(f).start()

        @pl.loop(1, members)
        def _(k):
            copy1(f, partner(k), k, me).start()

    send_pieces(0)
    send_pieces(1)
    send_pieces(2)
    got_place[me] = place_ref[...]

    @pl.loop(1, members)
    def _(k):
        place_copy((me + k) % members, k, (me + k) % members).wait_recv()

    lane8 = lax.broadcasted_iota(jnp.int32, (8, LANES), 1)
    row8 = lax.broadcasted_iota(jnp.int32, (8, LANES), 0)

    def find(src, total):
        here = (got_place[src] == lane8) & (row8 < 4)
        return jnp.maximum(total, jnp.where(here, src * 4 + row8, 0))

    owner = lax.fori_loop(0, members, find, jnp.zeros((8, LANES), jnp.int32))
    for shift in (4, 2, 1):
        owner = jnp.maximum(owner, pltpu.roll(owner, shift, 0))
    inv_vmem[...] = owner
    inv_copy = pltpu.make_async_copy(inv_vmem, inv_smem, inv_sem)
    inv_copy.start()
    inv_copy.wait()

    def forward(f):
        own1(f).wait()

        @pl.loop(1, members)
        def _(k):
            copy1(f, (me + k) % members, k, (me + k) % members).wait_recv()

        def pick(t, q):
            index = inv_smem[0, t * 4 + q]
            return got[f][index >> 2, pl.ds(index & 3, rows, stride=4), :]

        @pl.loop(1, members)
        def _(k):
            t = partner(k)
            for q in range(4):
                sorted_[f, t, q * rows:(q + 1) * rows, :] = pick(t, q)
            copy2(f, t, k, me).start()

        for q in range(4):
            final[f, me, q * rows:(q + 1) * rows, :] = pick(me, q)

    def unpack(f, out, first):
        def one(j):
            for slab in range(slabs):
                tiles = [final[f, j, q * rows + slab * 8:q * rows + slab * 8 + 8, :] for q in range(4)]
                for yr in range(4):
                    whole = tiles[yr]
                    for q in range(4):
                        if q != yr:
                            turned = pltpu.roll(tiles[q], (32 * (q - yr)) % LANES, 1)
                            whole = jnp.where(lane8 // 32 == q, turned, whole)
                    out[j * slabs + slab + first, pl.ds(yr, 8, stride=4), :] = whole

        one(me)

        @pl.loop(1, members)
        def _(k):
            j = sender(k)
            copy2(f, j, k, j).wait_recv()
            one(j)

    def exchange(e, field, planes, acts=("start", "wait")):
        for act in acts:
            if act == "only":
                continue
            for axis in (1, 0, 2):
                for side in range(2):
                    d = axis * 2 + side
                    place, count = ((gx, n_gx), (gy, n_gy), (gz, n_gz))[axis]
                    there = place > 0 if side == 0 else place < count - 1
                    other = [gx, gy, gz]
                    other[axis] = place + (2 * side - 1)
                    if axis == 0:
                        src, dst = field.at[1 if side == 0 else planes], hx
                        to, mine = dst.at[e, 1 - side], dst.at[e, side]
                    elif axis == 1:
                        src = ys.at[side, pl.ds(0, planes)]
                        to, mine = hy.at[e, 1 - side, pl.ds(0, planes)], hy.at[e, side, pl.ds(0, planes)]
                    else:
                        src, to, mine = zs, hz.at[e, 1 - side], hz.at[e, side]

                    @pl.when(there)
                    def _():
                        out = pltpu.make_async_remote_copy(
                            src_ref=src, dst_ref=to, send_sem=halo_send.at[d],
                            recv_sem=halo_recv.at[e, axis * 2 + 1 - side],
                            device_id=tuple(other), device_id_type=MESH,
                        )
                        if act == "start":
                            out.start()
                        else:
                            out.wait_send()
                            pltpu.make_async_remote_copy(
                                src_ref=src, dst_ref=mine, send_sem=halo_send.at[d],
                                recv_sem=halo_recv.at[e, d],
                                device_id=tuple(other), device_id_type=MESH,
                            ).wait_recv()
        if acts[-1] != "wait":
            return
        low, lane = field[1], lane_ids()
        field[0] = pltpu.roll(jnp.where(lane >= NZ, hx[e, 0], field[planes]), NZ, 1)
        field[planes + 1] = pltpu.roll(jnp.where(lane < NZ, hx[e, 1], low), NZ, 1)

    def level_pass(planes, st, body, staged=True, field=None, e=None, out_st=None):
        lane, row = lane_ids(), row_ids()
        out_st = st if out_st is None else out_st
        spot = ((lane + out_st) % NZ) // (2 * out_st)
        if e is not None:
            beyond = jnp.where((lane // st) % 2 == 0, hz[e, 1], pltpu.roll(hz[e, 0], 2 * st, 1))

        def step(g, packed):
            xs = [g * GROUP + i for i in range(GROUP)]
            hoods = [None] * GROUP
            if e is not None:
                loaded = [field[xs[0] + i] for i in range(GROUP + 2)]
                hoods = []
                for i in range(GROUP):
                    c = loaded[i + 1]
                    yl = jnp.where(row < st, hy[e, 0, pl.ds(xs[i], 1), :], pltpu.roll(c, st, 0))
                    yh = jnp.where(row >= NY - st, hy[e, 1, pl.ds(xs[i], 1), :], pltpu.roll(c, NY - st, 0))
                    w = pltpu.roll(beyond, (LANES + NZ - st - xs[i] * (2 * st)) % LANES, 1)
                    zl = jnp.where(lane % NZ < st, w, pltpu.roll(c, st, 1))
                    zh = jnp.where(lane % NZ >= NZ - st, w, pltpu.roll(c, LANES - st, 1))
                    hoods.append((c, loaded[i], loaded[i + 2], yl, yh, zl, zh))
            results = body(xs, hoods)
            if staged:
                places = [g * len(results) + i for i in range(len(results))]
                for x, n in zip(places, results):
                    packed = jnp.where(spot == x, pltpu.roll(n, x * (2 * out_st), 1), packed)
                for x, n in zip(places, results):
                    ys[0, pl.ds(x, 1), :] = n[0:1, :]
                    ys[1, pl.ds(x, 1), :] = n[NY - 1:NY, :]
            return packed

        if staged:
            zs[...] = lax.fori_loop(0, planes // GROUP, step, jnp.zeros((NY, LANES), F32))
        else:
            lax.fori_loop(0, planes // GROUP, step, 0)

    fine_faces = (fx, fyl, fyh, fzl, fzh, fye, fze)
    coarse_faces = (cfx, cfyl, cfyh, cfzl, cfzh, cfye, cfze)

    def split_faces(st, yl, yh, zl, zh):
        row, z = row_ids(), lane_ids() % NZ
        y_low, y_high, z_low, z_high = row < st, row >= NY - st, z < st, z >= NZ - st
        return (
            jnp.where(y_low, 0.0, yl), jnp.where(y_high, 0.0, yh),
            jnp.where(z_low, 0.0, zl), jnp.where(z_high, 0.0, zh),
            jnp.where(y_low, yl, jnp.where(y_high, yh, 0.0)),
            jnp.where(z_low, zl, jnp.where(z_high, zh, 0.0)),
        )

    def halo_pass(field, e, planes, st, faces, body, staged=True, out_st=None):
        across, yl, yh, zl, zh, ye, ze = faces
        exchange(e, field, planes, ("start",))
        lane = lane_ids()
        first, last = field[1], field[planes]
        field[0] = pltpu.roll(jnp.where(lane < NZ, last, 0.0), NZ, 1)
        field[planes + 1] = pltpu.roll(jnp.where(lane >= NZ, first, 0.0), NZ, 1)

        @pl.loop(0, planes // GROUP)
        def _(g):
            xs = [g * GROUP + i for i in range(GROUP)]
            loaded = [field[xs[0] + i] for i in range(GROUP + 2)]
            sums = []
            for i, x in enumerate(xs):
                c = loaded[i + 1]
                sums.append(
                    (across[x] * loaded[i] + across[x + 1] * loaded[i + 2])
                    + (yl[x] * pltpu.roll(c, st, 0) + yh[x] * pltpu.roll(c, NY - st, 0))
                    + (zl[x] * pltpu.roll(c, st, 1) + zh[x] * pltpu.roll(c, LANES - st, 1))
                )
            for x, total in zip(xs, sums):
                inner[x] = total

        exchange(e, field, planes, ("wait", "only"))
        inner[0] += across[0] * pltpu.roll(jnp.where(lane >= NZ, hx[e, 0], 0.0), NZ, 1)
        inner[planes - 1] += across[planes] * pltpu.roll(jnp.where(lane < NZ, hx[e, 1], 0.0), NZ, 1)
        beyond = jnp.where((lane // st) % 2 == 0, hz[e, 1], pltpu.roll(hz[e, 0], 2 * st, 1))
        lower = row_ids() < NY // 2

        def with_halos(xs, hoods):
            pairs = []
            for x in xs:
                w = pltpu.roll(beyond, (LANES + NZ - st - x * (2 * st)) % LANES, 1)
                y = jnp.where(lower, hy[e, 0, pl.ds(x, 1), :], hy[e, 1, pl.ds(x, 1), :])
                pairs.append((field[x + 1], inner[x] + (ye[x] * y + ze[x] * w)))
            return body(xs, pairs)

        level_pass(planes, st, with_halos, staged=staged, out_st=out_st)

    def is_colour(x, st, colour):
        return (row_ids() // st + lane_ids() // st + x + colour) % 2 == 0

    forward(0)
    forward(1)
    unpack(0, bv, 1)
    level_pass(PLANES, 1, lambda xs, hoods: [bv[x + 1] for x in xs])
    exchange(0, bv, PLANES, ("start",))
    forward(2)
    exchange(0, bv, PLANES, ("wait",))

    def faces(xs, hoods):
        for x, (c, xl, xh, yl, yh, zl, zh) in zip(xs, hoods):
            fx[x] = 0.5 * (c + xl)
            fyl[x] = 0.5 * (c + yl)
            fyh[x] = 0.5 * (c + yh)
            fzl[x] = 0.5 * (c + zl)
            fzh[x] = 0.5 * (c + zh)

    level_pass(PLANES, 1, faces, staged=False, field=bv, e=0)
    fx[PLANES] = 0.5 * (bv[PLANES] + bv[PLANES + 1])

    unpack(1, ac, 0)

    @pl.loop(0, PLANES // 2)
    def _(i):
        x = 2 * i
        for o in range(2):
            d = ac[x + o] + (
                (fx[x + o] + fx[x + o + 1]) + (fyl[x + o] + fyh[x + o]) + (fzl[x + o] + fzh[x + o])
            )
            dg[x + o] = d
            rd[x + o] = 1.0 / d
        s = 0.0625
        wxl = s * pair_z(pair_y(fx[x]))
        wxh = s * pair_z(pair_y(fx[x + 2]))
        wyl = s * pair_z(even_y(fyl[x] + fyl[x + 1]))
        wyh = s * pair_z(odd_y(fyh[x] + fyh[x + 1]))
        wzl = s * pair_y(even_z(fzl[x] + fzl[x + 1]))
        wzh = s * pair_y(odd_z(fzh[x] + fzh[x + 1]))
        cfx[i] = wxl
        cfx[i + 1] = wxh
        for ref, face in zip(coarse_faces[1:], split_faces(2, wyl, wyh, wzl, wzh)):
            ref[i] = face
        ca = 0.125 * pair_z(pair_y(ac[x] + ac[x + 1]))
        crd[i] = 1.0 / (ca + ((wxl + wxh) + (wyl + wyh) + (wzl + wzh)))
        for o in range(2):
            full = split_faces(1, fyl[x + o], fyh[x + o], fzl[x + o], fzh[x + o])
            for ref, face in zip(fine_faces[1:], full):
                ref[x + o] = face

    unpack(2, rh, 0)

    def store(field, xs, values):
        for x, n in zip(xs, values):
            field[x + 1] = n
        return values

    def first_red(xs, hoods):
        return store(v, xs, [jnp.where(is_colour(x, 1, 0), rh[x] * rd[x], 0.0) for x in xs])

    def half(e, colour):
        def update(xs, hoods):
            values = []
            for x, hood in zip(xs, hoods):
                c, nb = hood
                values.append(jnp.where(is_colour(x, 1, colour), (rh[x] + nb) * rd[x], c))
            return store(v, xs, values)

        halo_pass(v, e, PLANES, 1, fine_faces, update)

    level_pass(PLANES, 1, first_red)
    half(1, 1)

    def restrict(xs, hoods):
        values = []
        for p in range(0, GROUP, 2):
            total = None
            for x, hood in zip(xs[p:p + 2], hoods[p:p + 2]):
                c, nb = hood
                r = rh[x] - (dg[x] * c - nb)
                total = r if total is None else total + r
            values.append(0.125 * pair_z(pair_y(total)))
        places = [xs[0] // 2 + i for i in range(GROUP // 2)]
        for i, f in zip(places, values):
            cf[i] = f
        return store(
            cc, places,
            [jnp.where(is_colour(i, 2, 0), f * crd[i], 0.0) for i, f in zip(places, values)],
        )

    halo_pass(v, 2, PLANES, 1, fine_faces, restrict, out_st=2)

    def coarse_half(h, xs, hoods):
        values = []
        for x, hood in zip(xs, hoods):
            c, nb = hood
            values.append(jnp.where(is_colour(x, 2, h), (cf[x] + nb) * crd[x], c))
        return values

    @pl.loop(1, COARSE_HALVES - 1)
    def _(h):
        halo_pass(
            cc, 2 + h, PLANES // 2, 2, coarse_faces,
            lambda xs, hoods: store(cc, xs, coarse_half(h, xs, hoods)),
        )

    def correct(xs, hoods):
        values = []
        for x, n in zip(xs, coarse_half(COARSE_HALVES - 1, xs, hoods)):
            values += [v[2 * x + 1] + n, v[2 * x + 2] + n]
        return store(v, [2 * xs[0] + i for i in range(2 * GROUP)], values)

    halo_pass(cc, 9, PLANES // 2, 2, coarse_faces, correct, out_st=1)
    half(10, 0)
    half(11, 1)

    def finish(xs, hoods):
        for x, hood in zip(xs, hoods):
            c, nb = hood
            r = rh[x] - (dg[x] * c - nb)
            for out, n in ((sol_out, c), (res_out, r)):
                out[x] = n[:, :NZ]
                out[x + PLANES] = pltpu.roll(n, NZ, 1)[:, :NZ]

    halo_pass(v, 12, PLANES, 1, fine_faces, finish, staged=False)

    @pl.loop(1, members)
    def _(k):
        peer = partner(k)
        place_copy(peer, k, me).wait_send()
        for f in range(3):
            copy1(f, peer, k, me).wait_send()
            copy2(f, peer, k, me).wait_send()


def solution(mesh):
    sizes = (mesh.shape["gx"], mesh.shape["gy"], mesh.shape["gz"])
    members = sizes[0] * sizes[1]
    rows = 256 // members

    def rows128(boxes):
        return boxes[0].reshape(4, 256, LANES).transpose(1, 0, 2).reshape(1024, LANES)

    def body(rhs_boxes, a_boxes, b_boxes, new_place):
        spot = jnp.where(jnp.arange(8)[:, None] < 4, jnp.tile(new_place[0], 2)[:, None], -1)
        spot = jnp.broadcast_to(spot, (8, LANES)).astype(jnp.int32)
        fine = pltpu.VMEM((PLANES, NY, LANES), F32)
        coarse = pltpu.VMEM((PLANES // 2, NY, LANES), F32)
        box = pltpu.VMEM((members, 4 * rows, LANES), F32)
        boxes = pltpu.VMEM((3, members, 4 * rows, LANES), F32)
        dma = pltpu.SemaphoreType.DMA
        return pl.pallas_call(
            functools.partial(kernel, sizes),
            out_shape=[jax.ShapeDtypeStruct((NX, NY, NZ), F32)] * 2,
            in_specs=[pl.BlockSpec(memory_space=pltpu.VMEM)] + [pl.BlockSpec(memory_space=pltpu.HBM)] * 3,
            out_specs=[pl.BlockSpec(memory_space=pltpu.VMEM)] * 2,
            scratch_shapes=[
                pltpu.VMEM((members, 8, LANES), jnp.int32),
                pltpu.VMEM((8, LANES), jnp.int32),
                pltpu.SMEM((8, LANES), jnp.int32),
                box, box, box, boxes, boxes,
                pltpu.VMEM((PLANES + 2, NY, LANES), F32),
                fine, fine, fine, fine,
                pltpu.VMEM((PLANES + 1, NY, LANES), F32),
                fine, fine, fine, fine,
                pltpu.VMEM((PLANES + 2, NY, LANES), F32),
                pltpu.VMEM((PLANES // 2 + 2, NY, LANES), F32),
                coarse, coarse,
                pltpu.VMEM((PLANES // 2 + 1, NY, LANES), F32),
                coarse, coarse, coarse, coarse,
                fine, fine, coarse, coarse, fine,
                pltpu.VMEM((EXCHANGES, 2, NY, LANES), F32),
                pltpu.VMEM((EXCHANGES, 2, PLANES, LANES), F32),
                pltpu.VMEM((EXCHANGES, 2, NY, LANES), F32),
                pltpu.VMEM((2, PLANES, LANES), F32),
                pltpu.VMEM((NY, LANES), F32),
                dma((members,)), dma((members,)),
                dma((3, members)), dma((3, members)),
                dma((3, members)), dma((3, members)),
                dma,
                dma((6,)), dma((EXCHANGES, 6)),
            ],
            compiler_params=pltpu.CompilerParams(
                collective_id=0, has_side_effects=True, vmem_limit_bytes=60 * 1024 * 1024
            ),
        )(spot, rows128(rhs_boxes), rows128(a_boxes), rows128(b_boxes))

    return jax.shard_map(
        body,
        mesh=mesh,
        in_specs=(
            P("gz", ("gx", "gy"), None),
            P("gz", ("gx", "gy"), None),
            P("gz", ("gx", "gy"), None),
            P("gz", ("gx", "gy")),
        ),
        out_specs=(P("gx", "gy", "gz"), P("gx", "gy", "gz")),
        check_vma=False,
    )
```

```python
import functools

import jax
import jax.numpy as jnp
from jax import lax
from jax.experimental import pallas as pl
from jax.experimental.pallas import tpu as pltpu
from jax.sharding import PartitionSpec as P

MESH = pl.DeviceIdType.MESH
NX, NY, NZ = 64, 32, 64
PLANES = NX // 2
LANES = 128
COARSE_HALVES = 8
EXCHANGES = 13
GROUP = 8
F32 = jnp.float32


def lane_ids():
    return lax.broadcasted_iota(jnp.int32, (NY, LANES), 1)


def row_ids():
    return lax.broadcasted_iota(jnp.int32, (NY, LANES), 0)


def pair_z(v):
    return v + jnp.where(lane_ids() % 2 == 0, pltpu.roll(v, LANES - 1, 1), pltpu.roll(v, 1, 1))


def pair_y(v):
    return v + jnp.where(row_ids() % 2 == 0, pltpu.roll(v, NY - 1, 0), pltpu.roll(v, 1, 0))


def even_y(v):
    return jnp.where(row_ids() % 2 == 0, v, pltpu.roll(v, 1, 0))


def odd_y(v):
    return jnp.where(row_ids() % 2 == 1, v, pltpu.roll(v, NY - 1, 0))


def even_z(v):
    return jnp.where(lane_ids() % 2 == 0, v, pltpu.roll(v, 1, 1))


def odd_z(v):
    return jnp.where(lane_ids() % 2 == 1, v, pltpu.roll(v, LANES - 1, 1))


def kernel(
    sizes,
    place_ref, rhs_in, a_in, b_in,
    sol_out, res_out,
    got_place, inv_vmem, inv_smem, got_b, got_a, got_rhs, sorted_, final,
    bv, rh, ac, dg, rd, fx, fyl, fyh, fzl, fzh, v,
    cc, cf, crd, cfx, cfyl, cfyh, cfzl, cfzh,
    fye, fze, cfye, cfze, inner,
    hx, hy, hz, ys, zs,
    place_send, place_recv, send1, recv1, send2, recv2, inv_sem, halo_send, halo_recv,
):
    n_gx, n_gy, n_gz = sizes
    members = n_gx * n_gy
    rows = 256 // members
    slabs = rows // 8
    gx, gy, gz = lax.axis_index("gx"), lax.axis_index("gy"), lax.axis_index("gz")
    me = gx * n_gy + gy
    got = (got_b, got_a, got_rhs)

    def partner(k):
        return (me + 1 + (k + members // 2 - 2) % (members - 1)) % members

    def sender(k):
        return (me + members - 1 - (k + members // 2 - 2) % (members - 1)) % members

    def member(t):
        return (t // n_gy, t % n_gy, gz)

    @pl.loop(0, EXCHANGES)
    def _(e):
        for side in range(2):
            hx[e, side] = jnp.zeros((NY, LANES), F32)
            hy[e, side] = jnp.zeros((PLANES, LANES), F32)
            hz[e, side] = jnp.zeros((NY, LANES), F32)

    barrier = pltpu.get_barrier_semaphore()

    @pl.loop(1, members)
    def _(k):
        pl.semaphore_signal(barrier, inc=1, device_id=member((me + k) % members), device_id_type=MESH)

    @pl.when(gz > 0)
    def _():
        pl.semaphore_signal(barrier, inc=1, device_id=(gx, gy, gz - 1), device_id_type=MESH)

    @pl.when(gz < n_gz - 1)
    def _():
        pl.semaphore_signal(barrier, inc=1, device_id=(gx, gy, gz + 1), device_id_type=MESH)

    pl.semaphore_wait(
        barrier, members - 1 + (gz > 0).astype(jnp.int32) + (gz < n_gz - 1).astype(jnp.int32)
    )

    def place_copy(peer, k, slot):
        return pltpu.make_async_remote_copy(
            src_ref=place_ref, dst_ref=got_place.at[slot],
            send_sem=place_send.at[k], recv_sem=place_recv.at[slot],
            device_id=member(peer), device_id_type=MESH,
        )

    def copy1(f, peer, k, slot):
        return pltpu.make_async_remote_copy(
            src_ref=(b_in, a_in, rhs_in)[f].at[pl.ds(pl.multiple_of(peer * 4 * rows, 8), 4 * rows)],
            dst_ref=got[f].at[slot],
            send_sem=send1.at[f, k], recv_sem=recv1.at[f, slot],
            device_id=member(peer), device_id_type=MESH,
        )

    def copy2(f, peer, k, slot):
        return pltpu.make_async_remote_copy(
            src_ref=sorted_.at[f, peer], dst_ref=final.at[f, slot],
            send_sem=send2.at[f, k], recv_sem=recv2.at[f, slot],
            device_id=member(peer), device_id_type=MESH,
        )

    @pl.loop(1, members)
    def _(k):
        place_copy(partner(k), k, me).start()

    def own1(f):
        return pltpu.make_async_copy(
            (b_in, a_in, rhs_in)[f].at[pl.ds(pl.multiple_of(me * 4 * rows, 8), 4 * rows)],
            got[f].at[me], recv1.at[f, me],
        )

    def send_pieces(f):
        own1(f).start()

        @pl.loop(1, members)
        def _(k):
            copy1(f, partner(k), k, me).start()

    send_pieces(0)
    send_pieces(1)
    send_pieces(2)
    got_place[me] = place_ref[...]

    @pl.loop(1, members)
    def _(k):
        place_copy((me + k) % members, k, (me + k) % members).wait_recv()

    lane8 = lax.broadcasted_iota(jnp.int32, (8, LANES), 1)
    row8 = lax.broadcasted_iota(jnp.int32, (8, LANES), 0)

    def find(src, total):
        here = (got_place[src] == lane8) & (row8 < 4)
        return jnp.maximum(total, jnp.where(here, src * 4 + row8, 0))

    owner = lax.fori_loop(0, members, find, jnp.zeros((8, LANES), jnp.int32))
    for shift in (4, 2, 1):
        owner = jnp.maximum(owner, pltpu.roll(owner, shift, 0))
    inv_vmem[...] = owner
    inv_copy = pltpu.make_async_copy(inv_vmem, inv_smem, inv_sem)
    inv_copy.start()
    inv_copy.wait()

    def forward(f):
        own1(f).wait()

        @pl.loop(1, members)
        def _(k):
            copy1(f, (me + k) % members, k, (me + k) % members).wait_recv()

        def pick(t, q):
            index = inv_smem[0, t * 4 + q]
            return got[f][index >> 2, pl.ds(index & 3, rows, stride=4), :]

        @pl.loop(1, members)
        def _(k):
            t = partner(k)
            for q in range(4):
                sorted_[f, t, q * rows:(q + 1) * rows, :] = pick(t, q)
            copy2(f, t, k, me).start()

        for q in range(4):
            final[f, me, q * rows:(q + 1) * rows, :] = pick(me, q)

    def unpack(f, out, first):
        def one(j):
            for slab in range(slabs):
                tiles = [final[f, j, q * rows + slab * 8:q * rows + slab * 8 + 8, :] for q in range(4)]
                for yr in range(4):
                    whole = tiles[yr]
                    for q in range(4):
                        if q != yr:
                            turned = pltpu.roll(tiles[q], (32 * (q - yr)) % LANES, 1)
                            whole = jnp.where(lane8 // 32 == q, turned, whole)
                    out[j * slabs + slab + first, pl.ds(yr, 8, stride=4), :] = whole

        one(me)

        @pl.loop(1, members)
        def _(k):
            j = sender(k)
            copy2(f, j, k, j).wait_recv()
            one(j)

    def exchange(e, field, planes, acts=("start", "wait")):
        for act in acts:
            if act == "only":
                continue
            for axis in (1, 0, 2):
                for side in range(2):
                    d = axis * 2 + side
                    place, count = ((gx, n_gx), (gy, n_gy), (gz, n_gz))[axis]
                    there = place > 0 if side == 0 else place < count - 1
                    other = [gx, gy, gz]
                    other[axis] = place + (2 * side - 1)
                    if axis == 0:
                        src, dst = field.at[1 if side == 0 else planes], hx
                        to, mine = dst.at[e, 1 - side], dst.at[e, side]
                    elif axis == 1:
                        src = ys.at[side, pl.ds(0, planes)]
                        to, mine = hy.at[e, 1 - side, pl.ds(0, planes)], hy.at[e, side, pl.ds(0, planes)]
                    else:
                        src, to, mine = zs, hz.at[e, 1 - side], hz.at[e, side]

                    @pl.when(there)
                    def _():
                        out = pltpu.make_async_remote_copy(
                            src_ref=src, dst_ref=to, send_sem=halo_send.at[d],
                            recv_sem=halo_recv.at[e, axis * 2 + 1 - side],
                            device_id=tuple(other), device_id_type=MESH,
                        )
                        if act == "start":
                            out.start()
                        else:
                            out.wait_send()
                            pltpu.make_async_remote_copy(
                                src_ref=src, dst_ref=mine, send_sem=halo_send.at[d],
                                recv_sem=halo_recv.at[e, d],
                                device_id=tuple(other), device_id_type=MESH,
                            ).wait_recv()
        if acts[-1] != "wait":
            return
        low, lane = field[1], lane_ids()
        field[0] = pltpu.roll(jnp.where(lane >= NZ, hx[e, 0], field[planes]), NZ, 1)
        field[planes + 1] = pltpu.roll(jnp.where(lane < NZ, hx[e, 1], low), NZ, 1)

    def level_pass(planes, st, body, staged=True, field=None, e=None, out_st=None):
        lane, row = lane_ids(), row_ids()
        out_st = st if out_st is None else out_st
        spot = ((lane + out_st) % NZ) // (2 * out_st)
        if e is not None:
            beyond = jnp.where((lane // st) % 2 == 0, hz[e, 1], pltpu.roll(hz[e, 0], 2 * st, 1))

        def step(g, packed):
            xs = [g * GROUP + i for i in range(GROUP)]
            hoods = [None] * GROUP
            if e is not None:
                loaded = [field[xs[0] + i] for i in range(GROUP + 2)]
                hoods = []
                for i in range(GROUP):
                    c = loaded[i + 1]
                    yl = jnp.where(row < st, hy[e, 0, pl.ds(xs[i], 1), :], pltpu.roll(c, st, 0))
                    yh = jnp.where(row >= NY - st, hy[e, 1, pl.ds(xs[i], 1), :], pltpu.roll(c, NY - st, 0))
                    w = pltpu.roll(beyond, (LANES + NZ - st - xs[i] * (2 * st)) % LANES, 1)
                    zl = jnp.where(lane % NZ < st, w, pltpu.roll(c, st, 1))
                    zh = jnp.where(lane % NZ >= NZ - st, w, pltpu.roll(c, LANES - st, 1))
                    hoods.append((c, loaded[i], loaded[i + 2], yl, yh, zl, zh))
            results = body(xs, hoods)
            if staged:
                places = [g * len(results) + i for i in range(len(results))]
                for x, n in zip(places, results):
                    packed = jnp.where(spot == x, pltpu.roll(n, x * (2 * out_st), 1), packed)
                for x, n in zip(places, results):
                    ys[0, pl.ds(x, 1), :] = n[0:1, :]
                    ys[1, pl.ds(x, 1), :] = n[NY - 1:NY, :]
            return packed

        if staged:
            zs[...] = lax.fori_loop(0, planes // GROUP, step, jnp.zeros((NY, LANES), F32))
        else:
            lax.fori_loop(0, planes // GROUP, step, 0)

    fine_faces = (fx, fyl, fyh, fzl, fzh, fye, fze)
    coarse_faces = (cfx, cfyl, cfyh, cfzl, cfzh, cfye, cfze)

    def split_faces(st, yl, yh, zl, zh):
        row, z = row_ids(), lane_ids() % NZ
        y_low, y_high, z_low, z_high = row < st, row >= NY - st, z < st, z >= NZ - st
        return (
            jnp.where(y_low, 0.0, yl), jnp.where(y_high, 0.0, yh),
            jnp.where(z_low, 0.0, zl), jnp.where(z_high, 0.0, zh),
            jnp.where(y_low, yl, jnp.where(y_high, yh, 0.0)),
            jnp.where(z_low, zl, jnp.where(z_high, zh, 0.0)),
        )

    def halo_pass(field, e, planes, st, faces, body, staged=True, out_st=None):
        across, yl, yh, zl, zh, ye, ze = faces
        exchange(e, field, planes, ("start",))
        lane = lane_ids()
        first, last = field[1], field[planes]
        field[0] = pltpu.roll(jnp.where(lane < NZ, last, 0.0), NZ, 1)
        field[planes + 1] = pltpu.roll(jnp.where(lane >= NZ, first, 0.0), NZ, 1)

        @pl.loop(0, planes // GROUP)
        def _(g):
            xs = [g * GROUP + i for i in range(GROUP)]
            loaded = [field[xs[0] + i] for i in range(GROUP + 2)]
            sums = []
            for i, x in enumerate(xs):
                c = loaded[i + 1]
                sums.append(
                    (across[x] * loaded[i] + across[x + 1] * loaded[i + 2])
                    + (yl[x] * pltpu.roll(c, st, 0) + yh[x] * pltpu.roll(c, NY - st, 0))
                    + (zl[x] * pltpu.roll(c, st, 1) + zh[x] * pltpu.roll(c, LANES - st, 1))
                )
            for x, total in zip(xs, sums):
                inner[x] = total

        exchange(e, field, planes, ("wait", "only"))
        inner[0] += across[0] * pltpu.roll(jnp.where(lane >= NZ, hx[e, 0], 0.0), NZ, 1)
        inner[planes - 1] += across[planes] * pltpu.roll(jnp.where(lane < NZ, hx[e, 1], 0.0), NZ, 1)
        beyond = jnp.where((lane // st) % 2 == 0, hz[e, 1], pltpu.roll(hz[e, 0], 2 * st, 1))
        lower = row_ids() < NY // 2

        def with_halos(xs, hoods):
            pairs = []
            for x in xs:
                w = pltpu.roll(beyond, (LANES + NZ - st - x * (2 * st)) % LANES, 1)
                y = jnp.where(lower, hy[e, 0, pl.ds(x, 1), :], hy[e, 1, pl.ds(x, 1), :])
                pairs.append((field[x + 1], inner[x] + (ye[x] * y + ze[x] * w)))
            return body(xs, pairs)

        level_pass(planes, st, with_halos, staged=staged, out_st=out_st)

    def is_colour(x, st, colour):
        return (row_ids() // st + lane_ids() // st + x + colour) % 2 == 0

    forward(0)
    forward(1)
    unpack(0, bv, 1)
    level_pass(PLANES, 1, lambda xs, hoods: [bv[x + 1] for x in xs])
    exchange(0, bv, PLANES, ("start",))
    forward(2)
    exchange(0, bv, PLANES, ("wait",))

    def faces(xs, hoods):
        for x, (c, xl, xh, yl, yh, zl, zh) in zip(xs, hoods):
            fx[x] = 0.5 * (c + xl)
            fyl[x] = 0.5 * (c + yl)
            fyh[x] = 0.5 * (c + yh)
            fzl[x] = 0.5 * (c + zl)
            fzh[x] = 0.5 * (c + zh)

    level_pass(PLANES, 1, faces, staged=False, field=bv, e=0)
    fx[PLANES] = 0.5 * (bv[PLANES] + bv[PLANES + 1])

    unpack(1, ac, 0)

    @pl.loop(0, PLANES // 2)
    def _(i):
        x = 2 * i
        for o in range(2):
            d = ac[x + o] + (
                (fx[x + o] + fx[x + o + 1]) + (fyl[x + o] + fyh[x + o]) + (fzl[x + o] + fzh[x + o])
            )
            dg[x + o] = d
            rd[x + o] = 1.0 / d
        s = 0.0625
        wxl = s * pair_z(pair_y(fx[x]))
        wxh = s * pair_z(pair_y(fx[x + 2]))
        wyl = s * pair_z(even_y(fyl[x] + fyl[x + 1]))
        wyh = s * pair_z(odd_y(fyh[x] + fyh[x + 1]))
        wzl = s * pair_y(even_z(fzl[x] + fzl[x + 1]))
        wzh = s * pair_y(odd_z(fzh[x] + fzh[x + 1]))
        cfx[i] = wxl
        cfx[i + 1] = wxh
        for ref, face in zip(coarse_faces[1:], split_faces(2, wyl, wyh, wzl, wzh)):
            ref[i] = face
        ca = 0.125 * pair_z(pair_y(ac[x] + ac[x + 1]))
        crd[i] = 1.0 / (ca + ((wxl + wxh) + (wyl + wyh) + (wzl + wzh)))
        for o in range(2):
            full = split_faces(1, fyl[x + o], fyh[x + o], fzl[x + o], fzh[x + o])
            for ref, face in zip(fine_faces[1:], full):
                ref[x + o] = face

    unpack(2, rh, 0)

    def store(field, xs, values):
        for x, n in zip(xs, values):
            field[x + 1] = n
        return values

    def first_red(xs, hoods):
        return store(v, xs, [jnp.where(is_colour(x, 1, 0), rh[x] * rd[x], 0.0) for x in xs])

    def half(e, colour):
        def update(xs, hoods):
            values = []
            for x, hood in zip(xs, hoods):
                c, nb = hood
                values.append(jnp.where(is_colour(x, 1, colour), (rh[x] + nb) * rd[x], c))
            return store(v, xs, values)

        halo_pass(v, e, PLANES, 1, fine_faces, update)

    level_pass(PLANES, 1, first_red)
    half(1, 1)

    def restrict(xs, hoods):
        values = []
        for p in range(0, GROUP, 2):
            total = None
            for x, hood in zip(xs[p:p + 2], hoods[p:p + 2]):
                c, nb = hood
                r = rh[x] - (dg[x] * c - nb)
                total = r if total is None else total + r
            values.append(0.125 * pair_z(pair_y(total)))
        places = [xs[0] // 2 + i for i in range(GROUP // 2)]
        for i, f in zip(places, values):
            cf[i] = f
        return store(
            cc, places,
            [jnp.where(is_colour(i, 2, 0), f * crd[i], 0.0) for i, f in zip(places, values)],
        )

    halo_pass(v, 2, PLANES, 1, fine_faces, restrict, out_st=2)

    def coarse_half(h, xs, hoods):
        values = []
        for x, hood in zip(xs, hoods):
            c, nb = hood
            values.append(jnp.where(is_colour(x, 2, h), (cf[x] + nb) * crd[x], c))
        return values

    @pl.loop(1, COARSE_HALVES - 1)
    def _(h):
        halo_pass(
            cc, 2 + h, PLANES // 2, 2, coarse_faces,
            lambda xs, hoods: store(cc, xs, coarse_half(h, xs, hoods)),
        )

    def correct(xs, hoods):
        values = []
        for x, n in zip(xs, coarse_half(COARSE_HALVES - 1, xs, hoods)):
            values += [v[2 * x + 1] + n, v[2 * x + 2] + n]
        return store(v, [2 * xs[0] + i for i in range(2 * GROUP)], values)

    halo_pass(cc, 9, PLANES // 2, 2, coarse_faces, correct, out_st=1)
    half(10, 0)
    half(11, 1)

    def finish(xs, hoods):
        for x, hood in zip(xs, hoods):
            c, nb = hood
            r = rh[x] - (dg[x] * c - nb)
            for out, n in ((sol_out, c), (res_out, r)):
                out[x] = n

    halo_pass(v, 12, PLANES, 1, fine_faces, finish, staged=False)

    @pl.loop(1, members)
    def _(k):
        peer = partner(k)
        place_copy(peer, k, me).wait_send()
        for f in range(3):
            copy1(f, peer, k, me).wait_send()
            copy2(f, peer, k, me).wait_send()


def solution(mesh):
    sizes = (mesh.shape["gx"], mesh.shape["gy"], mesh.shape["gz"])
    members = sizes[0] * sizes[1]
    rows = 256 // members

    def rows128(boxes):
        return boxes[0].reshape(4, 256, LANES).transpose(1, 0, 2).reshape(1024, LANES)

    def body(rhs_boxes, a_boxes, b_boxes, new_place):
        spot = jnp.where(jnp.arange(8)[:, None] < 4, jnp.tile(new_place[0], 2)[:, None], -1)
        spot = jnp.broadcast_to(spot, (8, LANES)).astype(jnp.int32)
        fine = pltpu.VMEM((PLANES, NY, LANES), F32)
        coarse = pltpu.VMEM((PLANES // 2, NY, LANES), F32)
        box = pltpu.VMEM((members, 4 * rows, LANES), F32)
        boxes = pltpu.VMEM((3, members, 4 * rows, LANES), F32)
        dma = pltpu.SemaphoreType.DMA
        packed = pl.pallas_call(
            functools.partial(kernel, sizes),
            out_shape=[jax.ShapeDtypeStruct((PLANES, NY, LANES), F32)] * 2,
            in_specs=[pl.BlockSpec(memory_space=pltpu.VMEM)] + [pl.BlockSpec(memory_space=pltpu.HBM)] * 3,
            out_specs=[pl.BlockSpec(memory_space=pltpu.VMEM)] * 2,
            scratch_shapes=[
                pltpu.VMEM((members, 8, LANES), jnp.int32),
                pltpu.VMEM((8, LANES), jnp.int32),
                pltpu.SMEM((8, LANES), jnp.int32),
                box, box, box, boxes, boxes,
                pltpu.VMEM((PLANES + 2, NY, LANES), F32),
                fine, fine, fine, fine,
                pltpu.VMEM((PLANES + 1, NY, LANES), F32),
                fine, fine, fine, fine,
                pltpu.VMEM((PLANES + 2, NY, LANES), F32),
                pltpu.VMEM((PLANES // 2 + 2, NY, LANES), F32),
                coarse, coarse,
                pltpu.VMEM((PLANES // 2 + 1, NY, LANES), F32),
                coarse, coarse, coarse, coarse,
                fine, fine, coarse, coarse, fine,
                pltpu.VMEM((EXCHANGES, 2, NY, LANES), F32),
                pltpu.VMEM((EXCHANGES, 2, PLANES, LANES), F32),
                pltpu.VMEM((EXCHANGES, 2, NY, LANES), F32),
                pltpu.VMEM((2, PLANES, LANES), F32),
                pltpu.VMEM((NY, LANES), F32),
                dma((members,)), dma((members,)),
                dma((3, members)), dma((3, members)),
                dma((3, members)), dma((3, members)),
                dma,
                dma((6,)), dma((EXCHANGES, 6)),
            ],
            compiler_params=pltpu.CompilerParams(
                collective_id=0, has_side_effects=True, vmem_limit_bytes=60 * 1024 * 1024
            ),
        )(spot, rows128(rhs_boxes), rows128(a_boxes), rows128(b_boxes))
        return tuple(jnp.concatenate([p[..., :NZ], p[..., NZ:]], axis=0) for p in packed)

    return jax.shard_map(
        body,
        mesh=mesh,
        in_specs=(
            P("gz", ("gx", "gy"), None),
            P("gz", ("gx", "gy"), None),
            P("gz", ("gx", "gy"), None),
            P("gz", ("gx", "gy")),
        ),
        out_specs=(P("gx", "gy", "gz"), P("gx", "gy", "gz")),
        check_vma=False,
    )
```
